32 devices in a mesh: bucket: 8 (over z, x), entity: 4 (over y, core).
Axes of the slice: x: 2, y: 2, z: 4, core: 2. Of those that a mesh axis runs over, the one named last changes fastest.
Arguments:
- ent_table: bfloat16 [4096, 512], P('entity'), may hold values from -0.25 to 0.25
- panels: bfloat16 [32, 512, 512], P(('bucket', 'entity')), may hold values from -0.25 to 0.25
- rel_vecs: bfloat16 [32, 512], P(('bucket', 'entity')), may hold values from -0.19921875 to 0.19921875
- head_slots: int32 [32, 2, 128], P(('bucket', 'entity')), may hold values from 0 to 63
- tail_slots: int32 [32, 2, 128], P(('bucket', 'entity')), may hold values from 0 to 63
- negatives: int32 [32, 2, 512], P(('bucket', 'entity')), may hold values from 0 to 63
- requests: int32 [32, 4, 16], P(('bucket', 'entity')), may hold values from 0 to 1023, as said below
- block_count: int32 [32], P(('bucket', 'entity')), may hold values from 1 to 2, as said below
Outputs:
- ent_grad: float32 [4096, 512], P('entity', 'bucket')
- panel_grad: float32 [32, 512, 512], P(('bucket', 'entity'))
- rel_grad: float32 [32, 512], P(('bucket', 'entity'))
The draws below stay inside these ranges and needn't reach their ends.
Inputs may be any that keep to these rules, and one draw needn't show every extreme that they name: `requests`: for each device and row shard the 16 row numbers are distinct. `block_count`: at least one device has exactly 2 live blocks.
All inputs are finite; a program needn't handle non-finite values.
Results may differ from the reference program's by a relative error of at most 0.0095.
Values may be sent and summed in bfloat16 or wider, within the bound.
No kernel may reach another device: no remote copies, remote signals or barrier semaphores. Data moves between devices by JAX's collectives and lax.ppermute only.
A program may use at most 64 MiB of HBM per device.

```python
import jax
import jax.numpy as jnp
from jax import lax

D = 512
ENT_DEV = 1024
CAP = 16
BLK_MAX = 2
EDGE = 128
NEG = 512
ENT = 4096
REL = 32
N_BUCKET = 8
N_ENTITY = 4


def draw_requests(key, part):
    pair_count = N_BUCKET * N_ENTITY * N_ENTITY
    subkeys = jax.random.split(jax.random.fold_in(key, 11), pair_count)
    picked = jax.vmap(lambda subkey: jax.random.permutation(subkey, ENT_DEV)[:CAP])(subkeys)
    return picked.reshape(N_BUCKET * N_ENTITY, N_ENTITY, CAP).astype(jnp.int32)


def draw_block_count(key, part):
    device_total = N_BUCKET * N_ENTITY
    base = jax.random.fold_in(key, 23)
    first, second, third = jax.random.split(base, 3)
    picks = jax.random.randint(first, (device_total,), 0, 8)
    lower = jax.random.randint(second, (device_total,), 1, BLK_MAX // 2 + 1)
    counts = jnp.where(picks == 0, BLK_MAX, lower)
    hottest = jax.random.randint(third, (), 0, device_total)
    counts = jnp.where(jnp.arange(device_total) == hottest, BLK_MAX, counts)
    return counts.astype(jnp.int32)


def place_ends(result, key, low, high):
    longest = result.shape.index(max(result.shape))
    spots = []
    for shift in (0, 1):
        where = [jax.random.randint(jax.random.fold_in(key, axis), (), 0, length) for axis, length in enumerate(result.shape)]
        where[longest] = (where[longest] + shift) % result.shape[longest]
        spots.append(tuple(where))
    return result.at[spots[0]].set(low).at[spots[1]].set(high)


def levels(key, extent, shards, least, top_value):
    level = 1.0
    for axis_at, shards_of in shards:
        draws = jax.random.uniform(jax.random.fold_in(jax.random.fold_in(key, 6), axis_at), (shards_of,), jnp.float32, least / len(shards), top_value / len(shards))
        level = level * jnp.repeat(jnp.exp(draws), extent[axis_at] // shards_of).reshape((-1,) + (1,) * (len(extent) - 1 - axis_at))
    return level


def centred(own_key, shape, deviation, reach, cuts=(), held_as=jnp.bfloat16):
    result = deviation * jax.random.normal(own_key, shape, jnp.float32)
    if cuts:
        result = result * levels(own_key, shape, cuts, -0.22, 0.18)
    return jnp.clip(result, -reach, reach).astype(held_as)


def setup_inputs(seed: int = 0) -> dict:
    keys = jax.random.split(jax.random.key(seed), 9)
    ent_table = centred(keys[0], (ENT, D), D ** -0.5, 0.25, ((0, 4),))
    panels = centred(keys[1], (REL, D, D), D ** -0.5, 0.25, ((0, 32),))
    rel_vecs = centred(keys[2], (REL, D), 0.04, 0.19921875, ((0, 32),))
    head_slots = place_ends(jax.random.randint(keys[3], (N_BUCKET * N_ENTITY, BLK_MAX, EDGE), 0, N_ENTITY * CAP), jax.random.fold_in(keys[3], 1), 0, (N_ENTITY * CAP) - 1).astype(jnp.int32)
    tail_slots = place_ends(jax.random.randint(keys[4], (N_BUCKET * N_ENTITY, BLK_MAX, EDGE), 0, N_ENTITY * CAP), jax.random.fold_in(keys[4], 1), 0, (N_ENTITY * CAP) - 1).astype(jnp.int32)
    negatives = place_ends(jax.random.randint(keys[5], (N_BUCKET * N_ENTITY, BLK_MAX, NEG), 0, N_ENTITY * CAP), jax.random.fold_in(keys[5], 1), 0, (N_ENTITY * CAP) - 1).astype(jnp.int32)
    requests = draw_requests(jax.random.fold_in(keys[8], 71), 0)
    block_count = draw_block_count(jax.random.fold_in(keys[8], 71), 0)
    return {"ent_table": ent_table, "panels": panels, "rel_vecs": rel_vecs, "head_slots": head_slots, "tail_slots": tail_slots, "negatives": negatives, "requests": requests, "block_count": block_count}


MARGIN = 2.0


def device_terms(fetched, rel_panel, relation, head_one, tail_one, cand_one, live_mask):
    projected = jnp.dot(fetched, rel_panel.T, preferred_element_type=jnp.float32).astype(jnp.bfloat16)
    feature_count = projected.shape[1]
    head_rows = projected[head_one]
    tail_rows = projected[tail_one]
    cand_rows = projected[cand_one]
    centers = (head_rows.astype(jnp.float32) + relation.astype(jnp.float32)).astype(jnp.bfloat16)
    center_f = centers.astype(jnp.float32)
    tail_f = tail_rows.astype(jnp.float32)
    cand_f = cand_rows.astype(jnp.float32)
    offset = center_f - tail_f
    pos_dist = jnp.sum(offset * offset, -1)
    pos_weight = jax.nn.sigmoid(pos_dist - MARGIN) * live_mask[:, None]
    cross_terms = jnp.einsum("bed,bnd->ben", center_f, cand_f)
    neg_dist = jnp.sum(center_f * center_f, -1)[:, :, None] + jnp.sum(cand_f * cand_f, -1)[:, None, :] - 2.0 * cross_terms
    neg_weight = -jax.nn.sigmoid(MARGIN - neg_dist) / NEG * live_mask[:, None, None]
    weight_b = lax.optimization_barrier(neg_weight.astype(jnp.bfloat16)).astype(jnp.float32)
    grad_center = (2.0 * pos_weight[..., None] * offset
                   + 2.0 * jnp.sum(neg_weight, -1)[..., None] * center_f
                   - 2.0 * jnp.einsum("ben,bnd->bed", weight_b, cand_f))
    grad_tail = -2.0 * pos_weight[..., None] * offset
    grad_cand = (2.0 * jnp.sum(neg_weight, 1)[..., None] * cand_f
                 - 2.0 * jnp.einsum("ben,bed->bnd", weight_b, center_f))
    grad_proj = jnp.zeros(projected.shape, jnp.float32)
    grad_proj = grad_proj.at[head_one.reshape(-1)].add(grad_center.reshape(-1, feature_count))
    grad_proj = grad_proj.at[tail_one.reshape(-1)].add(grad_tail.reshape(-1, feature_count))
    grad_proj = grad_proj.at[cand_one.reshape(-1)].add(grad_cand.reshape(-1, feature_count))
    grad_rel = jnp.sum(grad_center, (0, 1))
    grad_proj_b = grad_proj.astype(jnp.bfloat16)
    grad_fetched = jnp.dot(grad_proj_b, rel_panel, preferred_element_type=jnp.float32)
    grad_panel = jnp.dot(grad_proj_b.T, fetched, preferred_element_type=jnp.float32)
    return grad_fetched, grad_panel, grad_rel


def reference(ent_table, panels, rel_vecs, head_slots, tail_slots, negatives, requests, block_count):
    device_total = N_BUCKET * N_ENTITY
    owners = jnp.arange(N_ENTITY, dtype=jnp.int32)[:, None] * ENT_DEV

    def visit(grad_table, device_index):
        row_numbers = (owners + requests[device_index]).reshape(-1).astype(jnp.int32)
        fetched = ent_table[row_numbers]
        live_mask = (jnp.arange(BLK_MAX, dtype=jnp.int32) < block_count[device_index]).astype(jnp.float32)
        grad_rows, grad_panel, grad_rel = device_terms(
            fetched, panels[device_index], rel_vecs[device_index],
            head_slots[device_index], tail_slots[device_index], negatives[device_index], live_mask)
        return grad_table.at[row_numbers].add(grad_rows), (grad_panel, grad_rel)

    grad_table, outputs = lax.scan(visit, jnp.zeros((ENT, D), jnp.float32),
                                   jnp.arange(device_total, dtype=jnp.int32))
    return grad_table, outputs[0], outputs[1]
```

```python
import jax
import jax.numpy as jnp
from jax import lax
from jax.experimental import pallas as pl
from jax.experimental.pallas import tpu as pltpu
from jax.sharding import PartitionSpec as P

MARGIN = 2.0
LANES = 128
DIGIT = 256
F32 = jnp.float32
BF16 = jnp.bfloat16
I32 = jnp.int32
VMEM_BYTES = 16 * 1024 * 1024


def dot(a, b, over):
    return lax.dot_general(a, b, ((over[:1], over[1:]), ((), ())), preferred_element_type=F32)


def iota(shape, axis):
    return lax.broadcasted_iota(I32, shape, axis)


def to_column(row_blocks):
    k = row_blocks[0].shape[1]
    tall = jnp.concatenate([jnp.broadcast_to(r, (k, k)) for r in row_blocks], axis=0)
    pick = lax.rem(iota(tall.shape, 0), k) == iota(tall.shape, 1)
    return jnp.sum(jnp.where(pick, tall, 0).astype(F32), axis=1, keepdims=True)


def flip(column):
    n = column.shape[0]
    return jnp.sum(jnp.where(iota((n, n), 0) == iota((n, n), 1), column, 0.0), axis=0, keepdims=True)


def flip_back(row):
    n = row.shape[1]
    return jnp.sum(jnp.where(iota((n, n), 0) == iota((n, n), 1), row, 0.0), axis=1, keepdims=True)


def call(kernel, outs, flops=0, nbytes=0):
    vmem = pl.BlockSpec(memory_space=pltpu.VMEM)
    smem = pl.BlockSpec(memory_space=pltpu.SMEM)

    def run(*args, scalars=()):
        return pl.pallas_call(
            kernel,
            out_shape=outs,
            in_specs=[smem] * len(scalars) + [vmem] * len(args),
            out_specs=[vmem] * len(outs),
            compiler_params=pltpu.CompilerParams(vmem_limit_bytes=VMEM_BYTES),
            cost_estimate=pl.CostEstimate(flops=flops, bytes_accessed=nbytes, transcendentals=0),
        )(*scalars, *args)

    return run


def counts_kernel(count_ref, head_ref, tail_ref, neg_ref, req_ref, edges_ref, pairs_ref, rows_ref):
    shards, cap = req_ref.shape[1:]
    total = shards * cap
    me = lax.axis_index("entity")
    blocks, edge = head_ref.shape[1:]
    negs = neg_ref.shape[2]
    live_blocks = count_ref[0]
    edges = jnp.zeros((total, total), F32)
    pairs = jnp.zeros((total, total), F32)
    edge_slot = jnp.bitwise_xor(iota((total, edge), 0), me * cap)
    neg_slot = jnp.bitwise_xor(iota((total, negs), 0), me * cap)
    for j in range(blocks):
        live = (j < live_blocks).astype(F32)
        head = (head_ref[0, j : j + 1, :] == edge_slot).astype(F32) * live
        tail = (tail_ref[0, j : j + 1, :] == edge_slot).astype(F32)
        neg = (neg_ref[0, j : j + 1, :] == neg_slot).astype(F32)
        edges += dot(head.astype(BF16), tail.astype(BF16), (1, 1))
        heads = jnp.sum(head, axis=1, keepdims=True)
        negatives = dot(jnp.ones((8, negs), BF16), neg.astype(BF16), (1, 1))[0:1]
        pairs += heads * negatives
    edges_ref[...] = edges
    pairs_ref[...] = pairs
    column = to_column([req_ref[0, pl.ds(jnp.bitwise_xor(me, s), 1), :] for s in range(shards)])
    high = jnp.floor(column * (1.0 / DIGIT))
    low = column - high * DIGIT
    rows_ref[...] = jnp.where(iota((total, LANES), 1) < 96, high, low)


def pick_kernel(*refs):
    table_ref, asked, outs = refs[0], refs[1 : 1 + (len(refs) - 1) // 2], refs[1 + (len(refs) - 1) // 2 :]
    me = lax.axis_index("entity")
    cap = asked[0].shape[2]
    column = to_column([r[0, pl.ds(me, 1), :] for r in asked]).astype(I32)
    rows = table_ref.shape[0]
    hot = (column == iota((column.shape[0], rows), 1)).astype(F32).astype(BF16)
    found = dot(hot, table_ref[...], (1, 0)).astype(BF16)
    for s, out in enumerate(outs):
        out[...] = found[s * cap : (s + 1) * cap]


def terms_kernel(buckets, negs, *refs):
    panel_ref, rel_ref, edges_ref, pairs_ref, rows_ref = refs[:5]
    send_ref, grad_ref, rel_grad_ref = refs[-3:]
    parts = refs[5:-3]
    shards = len(parts)
    fetched = jnp.concatenate([r[...] for r in parts], axis=0)
    panel = panel_ref[0]
    proj = dot(fetched, panel, (1, 1)).astype(BF16)
    proj_f = proj.astype(F32)
    centers = (proj_f + rel_ref[...].astype(F32)).astype(BF16)
    center_f = centers.astype(F32)
    cross = dot(centers, proj, (1, 1))
    dist = (
        jnp.sum(center_f * center_f, axis=1, keepdims=True)
        + flip(jnp.sum(proj_f * proj_f, axis=1, keepdims=True))
        - 2.0 * cross
    )
    pos = edges_ref[...] * jax.nn.sigmoid(dist - MARGIN)
    neg = -jax.nn.sigmoid(MARGIN - dist) * (1.0 / negs)
    exact = pos + pairs_ref[...] * neg
    rounded = pos + pairs_ref[...] * neg.astype(BF16).astype(F32)
    high = rounded.astype(BF16)
    low = (rounded - high.astype(F32)).astype(BF16)
    row_sum = jnp.sum(exact, axis=1, keepdims=True)
    col_sum = flip_back(jnp.sum(exact, axis=0, keepdims=True))
    grad_center = 2.0 * (row_sum * center_f - dot(high, proj, (1, 0)) - dot(low, proj, (1, 0)))
    grad_other = 2.0 * (col_sum * proj_f - dot(high, centers, (0, 0)) - dot(low, centers, (0, 0)))
    rel_grad_ref[...] = jnp.sum(grad_center, axis=0, keepdims=True)
    grad = (grad_center + grad_other).astype(BF16)
    grad_ref[...] = grad
    grad_rows = dot(grad, panel, (1, 0))
    total, features = grad_rows.shape
    cap = total // shards
    width = features // buckets
    me = lax.axis_index("entity")
    lane = iota((total, LANES), 1)
    for b in range(buckets):
        block, offset = divmod(b * width, LANES)
        piece = grad_rows[:, block * LANES : (block + 1) * LANES]
        if offset:
            piece = pltpu.roll(piece, LANES - offset, 1)
        piece = jnp.where(lane < width, piece, rows_ref[...]).astype(BF16)
        for s in range(shards):
            send_ref[b * shards + jnp.bitwise_xor(me, s)] = piece[s * cap : (s + 1) * cap]


def panel_kernel(grad_ref, *refs):
    fetched = jnp.concatenate([r[...] for r in refs[:-1]], axis=0)
    refs[-1][0] = dot(grad_ref[...], fetched, (0, 0))


def sum_kernel(width, got_ref, out_ref):
    devices, cap, _ = got_ref.shape
    rows = out_ref.shape[1]
    step = min(devices, 512 // cap)

    def part(i):
        got = got_ref[pl.ds(i * step, step)].reshape(step * cap, LANES)
        wide = got.astype(F32)
        column = (wide[:, 64:65] * DIGIT + wide[:, 96:97]).astype(I32)
        hot = (column == iota((step * cap, rows), 1)).astype(F32).astype(BF16)
        return dot(jnp.transpose(wide)[:width].astype(BF16), hot, (1, 0))

    if devices == step:
        out_ref[...] = part(0)
    else:
        out_ref[...] = jnp.zeros_like(out_ref)

        def add(i, _):
            out_ref[...] += part(i)
            return 0

        lax.fori_loop(0, devices // step, add, 0)


def body(ent_table, panels, rel_vecs, head_slots, tail_slots, negatives, requests, block_count):
    shards = lax.axis_size("entity")
    buckets = lax.axis_size("bucket")
    shard_rows, features = ent_table.shape
    cap = requests.shape[2]
    total = shards * cap
    width = features // buckets

    def swap(x, s):
        return lax.ppermute(x, "entity", [(i, i ^ s) for i in range(shards)])

    def out(shape, dtype=F32):
        return jax.ShapeDtypeStruct(shape, dtype)

    asked = [requests] + [swap(requests, s) for s in range(1, shards)]
    edges, pairs, rows = call(
        counts_kernel, [out((total, total)), out((total, total)), out((total, LANES))]
    )(head_slots, tail_slots, negatives, requests, scalars=(block_count,))
    found = call(pick_kernel, [out((cap, features), BF16)] * shards)(ent_table, *asked)
    parts = [found[0]] + [swap(found[s], s) for s in range(1, shards)]
    send, grad, rel_grad = call(
        lambda *refs: terms_kernel(buckets, negatives.shape[2], *refs),
        [out((buckets * shards, cap, LANES), BF16), out((total, features), BF16), out((1, features))],
    )(panels, rel_vecs, edges, pairs, rows, *parts)
    got = lax.all_to_all(send, ("bucket", "entity"), split_axis=0, concat_axis=0, tiled=True)
    [panel_grad] = call(
        panel_kernel, [out((1, features, features))], 2 * total * features * features, 4 * features * features
    )(grad, *parts)
    [ent_grad] = call(lambda *refs: sum_kernel(width, *refs), [out((width, shard_rows))])(got)
    return ent_grad.T, panel_grad, rel_grad


def solution(mesh):
    both = ("bucket", "entity")
    placed = (
        P("entity", None),
        P(both, None, None),
        P(both, None),
        P(both, None, None),
        P(both, None, None),
        P(both, None, None),
        P(both, None, None),
        P(both),
    )
    return jax.shard_map(
        body,
        mesh=mesh,
        in_specs=placed,
        out_specs=(P("entity", "bucket"), P(both, None, None), P(both, None)),
        check_vma=False,
    )
```

```python
import jax
import jax.numpy as jnp
from jax import lax
from jax.experimental import pallas as pl
from jax.experimental.pallas import tpu as pltpu
from jax.sharding import PartitionSpec as P

MARGIN = 2.0
LANES = 128
DIGIT = 256
F32 = jnp.float32
BF16 = jnp.bfloat16
I32 = jnp.int32
VMEM_BYTES = 16 * 1024 * 1024


def dot(a, b, over):
    return lax.dot_general(a, b, ((over[:1], over[1:]), ((), ())), preferred_element_type=F32)


def iota(shape, axis):
    return lax.broadcasted_iota(I32, shape, axis)


def to_column(row_blocks):
    k = row_blocks[0].shape[1]
    tall = jnp.concatenate([jnp.broadcast_to(r, (k, k)) for r in row_blocks], axis=0)
    pick = lax.rem(iota(tall.shape, 0), k) == iota(tall.shape, 1)
    return jnp.sum(jnp.where(pick, tall, 0).astype(F32), axis=1, keepdims=True)


def flip(column):
    n = column.shape[0]
    return jnp.sum(jnp.where(iota((n, n), 0) == iota((n, n), 1), column, 0.0), axis=0, keepdims=True)


def flip_back(row):
    n = row.shape[1]
    return jnp.sum(jnp.where(iota((n, n), 0) == iota((n, n), 1), row, 0.0), axis=1, keepdims=True)


def call(kernel, ins, outs, scratch=(), flops=0, nbytes=0):
    return pl.pallas_call(
        kernel,
        out_shape=outs,
        in_specs=[pl.BlockSpec(memory_space=space) for space in ins],
        out_specs=[pl.BlockSpec(memory_space=pltpu.VMEM)] * len(outs),
        scratch_shapes=list(scratch),
        compiler_params=pltpu.CompilerParams(vmem_limit_bytes=VMEM_BYTES),
        cost_estimate=pl.CostEstimate(flops=flops, bytes_accessed=nbytes, transcendentals=0),
    )


def prepare_kernel(
    count_ref, head_hbm, tail_hbm, neg_hbm, req_hbm, table_hbm, panel_hbm, rel_hbm,
    edges_ref, pairs_ref, rows_ref, req_ref, table_ref, panel_ref, rel_ref,
    head_ref, tail_ref, neg_ref, sems,
):
    moves = [
        pltpu.make_async_copy(src, dst, sems.at[i])
        for i, (src, dst) in enumerate(
            [
                (head_hbm, head_ref),
                (tail_hbm, tail_ref),
                (neg_hbm, neg_ref),
                (req_hbm, req_ref),
                (rel_hbm, rel_ref),
                (table_hbm, table_ref),
                (panel_hbm, panel_ref),
            ]
        )
    ]
    for move in moves:
        move.start()
    for move in moves[:4]:
        move.wait()
    shards, cap = req_ref.shape[1:]
    total = shards * cap
    me = lax.axis_index("entity")
    blocks, edge = head_ref.shape[1:]
    negs = neg_ref.shape[2]
    live_blocks = count_ref[0]
    edges = jnp.zeros((total, total), F32)
    pairs = jnp.zeros((total, total), F32)
    edge_slot = jnp.bitwise_xor(iota((total, edge), 0), me * cap)
    neg_slot = jnp.bitwise_xor(iota((total, negs), 0), me * cap)
    for j in range(blocks):
        live = (j < live_blocks).astype(F32)
        head = (head_ref[0, j : j + 1, :] == edge_slot).astype(F32) * live
        tail = (tail_ref[0, j : j + 1, :] == edge_slot).astype(F32)
        neg = (neg_ref[0, j : j + 1, :] == neg_slot).astype(F32)
        edges += dot(head.astype(BF16), tail.astype(BF16), (1, 1))
        heads = jnp.sum(head, axis=1, keepdims=True)
        negatives = dot(jnp.ones((8, negs), BF16), neg.astype(BF16), (1, 1))[0:1]
        pairs += heads * negatives
    edges_ref[...] = edges
    pairs_ref[...] = pairs
    column = to_column([req_ref[0, pl.ds(jnp.bitwise_xor(me, s), 1), :] for s in range(shards)])
    high = jnp.floor(column * (1.0 / DIGIT))
    low = column - high * DIGIT
    rows_ref[...] = jnp.where(iota((total, LANES), 1) < 96, high, low)
    for move in moves[4:]:
        move.wait()


def pick_kernel(*refs):
    table_ref, asked, outs = refs[0], refs[1 : 1 + (len(refs) - 1) // 2], refs[1 + (len(refs) - 1) // 2 :]
    me = lax.axis_index("entity")
    cap = asked[0].shape[2]
    column = to_column([r[0, pl.ds(me, 1), :] for r in asked]).astype(I32)
    rows = table_ref.shape[0]
    hot = (column == iota((column.shape[0], rows), 1)).astype(F32).astype(BF16)
    found = dot(hot, table_ref[...], (1, 0)).astype(BF16)
    for s, out in enumerate(outs):
        out[...] = found[s * cap : (s + 1) * cap]


def terms_kernel(buckets, negs, *refs):
    panel_ref, rel_ref, edges_ref, pairs_ref, rows_ref = refs[:5]
    send_ref, grad_ref, rel_grad_ref = refs[-3:]
    parts = refs[5:-3]
    shards = len(parts)
    fetched = jnp.concatenate([r[...] for r in parts], axis=0)
    panel = panel_ref[0]
    proj = dot(fetched, panel, (1, 1)).astype(BF16)
    proj_f = proj.astype(F32)
    centers = (proj_f + rel_ref[...].astype(F32)).astype(BF16)
    center_f = centers.astype(F32)
    cross = dot(centers, proj, (1, 1))
    dist = (
        jnp.sum(center_f * center_f, axis=1, keepdims=True)
        + flip(jnp.sum(proj_f * proj_f, axis=1, keepdims=True))
        - 2.0 * cross
    )
    pos = edges_ref[...] * jax.nn.sigmoid(dist - MARGIN)
    neg = -jax.nn.sigmoid(MARGIN - dist) * (1.0 / negs)
    exact = pos + pairs_ref[...] * neg
    rounded = pos + pairs_ref[...] * neg.astype(BF16).astype(F32)
    high = rounded.astype(BF16)
    low = (rounded - high.astype(F32)).astype(BF16)
    row_sum = jnp.sum(exact, axis=1, keepdims=True)
    col_sum = flip_back(jnp.sum(exact, axis=0, keepdims=True))
    grad_center = 2.0 * (row_sum * center_f - dot(high, proj, (1, 0)) - dot(low, proj, (1, 0)))
    grad_other = 2.0 * (col_sum * proj_f - dot(high, centers, (0, 0)) - dot(low, centers, (0, 0)))
    rel_grad_ref[...] = jnp.sum(grad_center, axis=0, keepdims=True)
    grad = (grad_center + grad_other).astype(BF16)
    grad_ref[...] = grad
    grad_rows = dot(grad, panel, (1, 0))
    total, features = grad_rows.shape
    cap = total // shards
    width = features // buckets
    me = lax.axis_index("entity")
    lane = iota((total, LANES), 1)
    for b in range(buckets):
        block, offset = divmod(b * width, LANES)
        piece = grad_rows[:, block * LANES : (block + 1) * LANES]
        if offset:
            piece = pltpu.roll(piece, LANES - offset, 1)
        piece = jnp.where(lane < width, piece, rows_ref[...]).astype(BF16)
        for s in range(shards):
            send_ref[b * shards + jnp.bitwise_xor(me, s)] = piece[s * cap : (s + 1) * cap]


def panel_kernel(grad_ref, *refs):
    fetched = jnp.concatenate([r[...] for r in refs[:-1]], axis=0)
    refs[-1][0] = dot(grad_ref[...], fetched, (0, 0))


def sum_kernel(width, got_ref, out_ref):
    devices, cap, _ = got_ref.shape
    rows = out_ref.shape[1]
    step = min(devices, 512 // cap)

    def part(i):
        got = got_ref[pl.ds(i * step, step)].reshape(step * cap, LANES)
        wide = got.astype(F32)
        column = (wide[:, 64:65] * DIGIT + wide[:, 96:97]).astype(I32)
        hot = (column == iota((step * cap, rows), 1)).astype(F32).astype(BF16)
        return dot(jnp.transpose(wide)[:width].astype(BF16), hot, (1, 0))

    if devices == step:
        out_ref[...] = part(0)
    else:
        out_ref[...] = jnp.zeros_like(out_ref)

        def add(i, _):
            out_ref[...] += part(i)
            return 0

        lax.fori_loop(0, devices // step, add, 0)


def body(ent_table, panels, rel_vecs, head_slots, tail_slots, negatives, requests, block_count):
    shards = lax.axis_size("entity")
    buckets = lax.axis_size("bucket")
    shard_rows, features = ent_table.shape
    cap = requests.shape[2]
    total = shards * cap
    width = features // buckets

    def swap(x, s):
        return lax.ppermute(x, "entity", [(i, i ^ s) for i in range(shards)])

    def out(shape, dtype=F32):
        return jax.ShapeDtypeStruct(shape, dtype)

    def like(x):
        return out(x.shape, x.dtype)

    vmem, hbm = pltpu.VMEM, pltpu.HBM
    asked = [swap(requests, s) for s in range(1, shards)]
    edges, pairs, rows, own, table, panel, rel = call(
        prepare_kernel,
        [pltpu.SMEM] + [hbm] * 7,
        [out((total, total)), out((total, total)), out((total, LANES))]
        + [like(x) for x in (requests, ent_table, panels, rel_vecs)],
        [
            pltpu.VMEM(head_slots.shape, I32),
            pltpu.VMEM(tail_slots.shape, I32),
            pltpu.VMEM(negatives.shape, I32),
            pltpu.SemaphoreType.DMA((7,)),
        ],
    )(
        block_count,
        *[
            pltpu.with_memory_space_constraint(x, hbm)
            for x in (head_slots, tail_slots, negatives, requests, ent_table, panels, rel_vecs)
        ]
    )
    found = call(pick_kernel, [vmem] * (1 + shards), [out((cap, features), BF16)] * shards)(table, own, *asked)
    parts = [found[0]] + [swap(found[s], s) for s in range(1, shards)]
    send, grad, rel_grad = call(
        lambda *refs: terms_kernel(buckets, negatives.shape[2], *refs),
        [vmem] * (5 + shards),
        [out((buckets * shards, cap, LANES), BF16), out((total, features), BF16), out((1, features))],
    )(panel, rel, edges, pairs, rows, *parts)
    got = lax.all_to_all(send, ("bucket", "entity"), split_axis=0, concat_axis=0, tiled=True)
    [panel_grad] = call(
        panel_kernel,
        [vmem] * (1 + shards),
        [out((1, features, features))],
        flops=2 * total * features * features,
        nbytes=4 * features * features,
    )(grad, *parts)
    [ent_grad] = call(lambda *refs: sum_kernel(width, *refs), [vmem], [out((width, shard_rows))])(got)
    return ent_grad.T, panel_grad, rel_grad


def solution(mesh):
    both = ("bucket", "entity")
    placed = (
        P("entity", None),
        P(both, None, None),
        P(both, None),
        P(both, None, None),
        P(both, None, None),
        P(both, None, None),
        P(both, None, None),
        P(both),
    )
    return jax.shard_map(
        body,
        mesh=mesh,
        in_specs=placed,
        out_specs=(P("entity", "bucket"), P(both, None, None), P(both, None)),
        check_vma=False,
    )
```

```python
import functools

import jax
import jax.numpy as jnp
from jax import lax
from jax.experimental import pallas as pl
from jax.experimental.pallas import tpu as pltpu
from jax.sharding import PartitionSpec as P

MARGIN = 2.0
LANES = 128
DIGIT = 256
F32 = jnp.float32
BF16 = jnp.bfloat16
I32 = jnp.int32
VMEM_BYTES = 16 * 1024 * 1024


def dot(a, b, over):
    return lax.dot_general(a, b, ((over[:1], over[1:]), ((), ())), preferred_element_type=F32)


def iota(shape, axis):
    return lax.broadcasted_iota(I32, shape, axis)


def to_column(row_blocks):
    k = row_blocks[0].shape[1]
    tall = jnp.concatenate([jnp.broadcast_to(r, (k, k)) for r in row_blocks], axis=0)
    pick = lax.rem(iota(tall.shape, 0), k) == iota(tall.shape, 1)
    return jnp.sum(jnp.where(pick, tall, 0).astype(F32), axis=1, keepdims=True)


def flip(column):
    n = column.shape[0]
    return jnp.sum(jnp.where(iota((n, n), 0) == iota((n, n), 1), column, 0.0), axis=0, keepdims=True)


def flip_back(row):
    n = row.shape[1]
    return jnp.sum(jnp.where(iota((n, n), 0) == iota((n, n), 1), row, 0.0), axis=1, keepdims=True)


def call(kernel, ins, outs, scratch=(), space=pltpu.VMEM):
    return pl.pallas_call(
        kernel,
        out_shape=outs,
        in_specs=[pl.BlockSpec(memory_space=place) for place in ins],
        out_specs=[pl.BlockSpec(memory_space=space)] * len(outs),
        scratch_shapes=list(scratch),
        compiler_params=pltpu.CompilerParams(vmem_limit_bytes=VMEM_BYTES),
    )


def prepare_kernel(
    count_ref, head_hbm, tail_hbm, neg_hbm, req_hbm, table_hbm, panel_hbm, rel_hbm,
    edges_ref, pairs_ref, rows_ref, req_ref, table_ref, panel_ref, rel_ref,
    head_ref, tail_ref, neg_ref, sems,
):
    moves = [
        pltpu.make_async_copy(src, dst, sems.at[i])
        for i, (src, dst) in enumerate(
            [
                (head_hbm, head_ref),
                (tail_hbm, tail_ref),
                (neg_hbm, neg_ref),
                (req_hbm, req_ref),
                (rel_hbm, rel_ref),
                (table_hbm, table_ref),
                (panel_hbm, panel_ref),
            ]
        )
    ]
    for move in moves:
        move.start()
    for move in moves[:4]:
        move.wait()
    shards, cap = req_ref.shape[1:]
    total = shards * cap
    me = lax.axis_index("entity")
    blocks, edge = head_ref.shape[1:]
    negs = neg_ref.shape[2]
    live_blocks = count_ref[0]
    edges = jnp.zeros((total, total), F32)
    pairs = jnp.zeros((total, total), F32)
    edge_slot = jnp.bitwise_xor(iota((total, edge), 0), me * cap)
    neg_slot = jnp.bitwise_xor(iota((total, negs), 0), me * cap)
    for j in range(blocks):
        live = (j < live_blocks).astype(F32)
        head = (head_ref[0, j : j + 1, :] == edge_slot).astype(F32) * live
        tail = (tail_ref[0, j : j + 1, :] == edge_slot).astype(F32)
        neg = (neg_ref[0, j : j + 1, :] == neg_slot).astype(F32)
        edges += dot(head.astype(BF16), tail.astype(BF16), (1, 1))
        heads = jnp.sum(head, axis=1, keepdims=True)
        negatives = dot(jnp.ones((8, negs), BF16), neg.astype(BF16), (1, 1))[0:1]
        pairs += heads * negatives
    edges_ref[...] = edges
    pairs_ref[...] = pairs
    column = to_column([req_ref[0, pl.ds(jnp.bitwise_xor(me, s), 1), :] for s in range(shards)])
    high = jnp.floor(column * (1.0 / DIGIT))
    low = column - high * DIGIT
    rows_ref[...] = jnp.where(iota((total, LANES), 1) < 96, high, low)
    for move in moves[4:]:
        move.wait()


def pick_kernel(first, near_ref, other_ref, asked_ref, out_ref):
    me = lax.axis_index("entity")
    cap = asked_ref.shape[2]
    for k, table_ref in enumerate((near_ref, other_ref)):
        column = to_column([asked_ref[0, pl.ds(jnp.bitwise_xor(me, k), 1), :]]).astype(I32)
        hot = (column == iota((cap, table_ref.shape[0]), 1)).astype(F32).astype(BF16)
        at = (first ^ k) * cap
        out_ref[at : at + cap] = dot(hot, table_ref[...], (1, 0)).astype(BF16)


def terms_kernel(buckets, negs, *refs):
    panel_ref, rel_ref, edges_ref, pairs_ref, rows_ref = refs[:5]
    send_ref, grad_ref, rel_grad_ref = refs[-3:]
    parts = refs[5:-3]
    fetched = jnp.concatenate([r[...] for r in parts], axis=0)
    panel = panel_ref[0]
    proj = dot(fetched, panel, (1, 1)).astype(BF16)
    proj_f = proj.astype(F32)
    centers = (proj_f + rel_ref[...].astype(F32)).astype(BF16)
    center_f = centers.astype(F32)
    cross = dot(centers, proj, (1, 1))
    dist = (
        jnp.sum(center_f * center_f, axis=1, keepdims=True)
        + flip(jnp.sum(proj_f * proj_f, axis=1, keepdims=True))
        - 2.0 * cross
    )
    pos = edges_ref[...] * jax.nn.sigmoid(dist - MARGIN)
    neg = -jax.nn.sigmoid(MARGIN - dist) * (1.0 / negs)
    exact = pos + pairs_ref[...] * neg
    rounded = pos + pairs_ref[...] * neg.astype(BF16).astype(F32)
    high = rounded.astype(BF16)
    low = (rounded - high.astype(F32)).astype(BF16)
    row_sum = jnp.sum(exact, axis=1, keepdims=True)
    col_sum = flip_back(jnp.sum(exact, axis=0, keepdims=True))
    grad_center = 2.0 * (row_sum * center_f - dot(high, proj, (1, 0)) - dot(low, proj, (1, 0)))
    grad_other = 2.0 * (col_sum * proj_f - dot(high, centers, (0, 0)) - dot(low, centers, (0, 0)))
    rel_grad_ref[...] = jnp.sum(grad_center, axis=0, keepdims=True)
    grad = (grad_center + grad_other).astype(BF16)
    grad_ref[...] = grad
    grad_rows = dot(grad, panel, (1, 0))
    total, features = grad_rows.shape
    shards, cap, _ = send_ref.shape
    shards //= buckets
    width = features // buckets
    me = lax.axis_index("entity")
    lane = iota((total, LANES), 1)
    for b in range(buckets):
        block, offset = divmod(b * width, LANES)
        piece = grad_rows[:, block * LANES : (block + 1) * LANES]
        if offset:
            piece = pltpu.roll(piece, LANES - offset, 1)
        piece = jnp.where(lane < width, piece, rows_ref[...]).astype(BF16)
        for s in range(shards):
            send_ref[b * shards + jnp.bitwise_xor(me, s)] = piece[s * cap : (s + 1) * cap]


def finish_kernel(width, got_ref, rel_grad_ref, grad_ref, *refs):
    parts, (sums_hbm, panel_hbm, rel_hbm, out_ref, panel_ref, sems) = refs[:-6], refs[-6:]
    fetched = jnp.concatenate([r[...] for r in parts], axis=0)
    moves = [pltpu.make_async_copy(rel_grad_ref, rel_hbm, sems.at[0])]
    moves[0].start()
    features = fetched.shape[1]
    half = features // 2
    for i in range(2):
        at = pl.ds(i * half, half)
        panel_ref[at] = dot(grad_ref[:, i * half : (i + 1) * half], fetched, (0, 0))
        moves.append(pltpu.make_async_copy(panel_ref.at[at], panel_hbm.at[0, at], sems.at[1 + i]))
        moves[-1].start()
    devices, cap, _ = got_ref.shape
    rows = out_ref.shape[1]
    step = min(devices, 512 // cap)
    count = step * cap

    def part(i):
        flat = jnp.transpose(got_ref[pl.ds(i * step, step)].reshape(count, LANES).astype(F32))
        values = flat[:width].astype(BF16)
        high, low = flat[64:65], flat[96:97]
        hot = (low.astype(I32) == iota((DIGIT, count), 0)).astype(F32).astype(BF16)
        kept = [values * (high == float(h)).astype(F32).astype(BF16) for h in range(rows // DIGIT)]
        return dot(jnp.concatenate(kept, axis=0), hot, (1, 1))

    def store(sums, add):
        for h in range(rows // DIGIT):
            piece = sums[h * width : (h + 1) * width]
            at = slice(h * DIGIT, (h + 1) * DIGIT)
            out_ref[:, at] = out_ref[:, at] + piece if add else piece

    store(part(0), False)
    if devices > step:

        def more(i, _):
            store(part(i), True)
            return 0

        lax.fori_loop(1, devices // step, more, 0)
    moves.append(pltpu.make_async_copy(out_ref, sums_hbm, sems.at[3]))
    moves[-1].start()
    for move in moves:
        move.wait()


def body(ent_table, panels, rel_vecs, head_slots, tail_slots, negatives, requests, block_count):
    shards = lax.axis_size("entity")
    buckets = lax.axis_size("bucket")
    shard_rows, features = ent_table.shape
    cap = requests.shape[2]
    total = shards * cap
    width = features // buckets

    def swap(x, s):
        return lax.ppermute(x, "entity", [(i, i ^ s) for i in range(shards)])

    def out(shape, dtype=F32):
        return jax.ShapeDtypeStruct(shape, dtype)

    def like(x):
        return out(x.shape, x.dtype)

    vmem, hbm = pltpu.VMEM, pltpu.HBM
    asked = [swap(requests, s) for s in range(3, shards, 2)]
    other = swap(ent_table, 1)
    edges, pairs, rows, own, table, panel, rel = call(
        prepare_kernel,
        [pltpu.SMEM] + [hbm] * 7,
        [out((total, total)), out((total, total)), out((total, LANES))]
        + [like(x) for x in (requests, ent_table, panels, rel_vecs)],
        [
            pltpu.VMEM(head_slots.shape, I32),
            pltpu.VMEM(tail_slots.shape, I32),
            pltpu.VMEM(negatives.shape, I32),
            pltpu.SemaphoreType.DMA((7,)),
        ],
    )(
        block_count,
        *[
            pltpu.with_memory_space_constraint(x, hbm)
            for x in (head_slots, tail_slots, negatives, requests, ent_table, panels, rel_vecs)
        ]
    )

    def pick(first, ids):
        kernel = functools.partial(pick_kernel, first)
        return call(kernel, [vmem] * 3, [out((2 * cap, features), BF16)])(table, other, ids)[0]

    found = [pick(1, ids) for ids in asked]
    parts = [pick(0, own)] + [swap(x, 2 * c + 3) for c, x in enumerate(found)]
    send, grad, rel_grad = call(
        lambda *refs: terms_kernel(buckets, negatives.shape[2], *refs),
        [vmem] * (5 + len(parts)),
        [out((buckets * shards, cap, LANES), BF16), out((total, features), BF16), out((1, features))],
    )(panel, rel, edges, pairs, rows, *parts)
    got = lax.all_to_all(send, ("bucket", "entity"), split_axis=0, concat_axis=0, tiled=True)
    ent_grad, panel_grad, rel_grad = call(
        functools.partial(finish_kernel, width),
        [vmem] * (3 + len(parts)),
        [out((width, shard_rows)), out((1, features, features)), out((1, features))],
        [
            pltpu.VMEM((width, shard_rows), F32),
            pltpu.VMEM((features, features), F32),
            pltpu.SemaphoreType.DMA((4,)),
        ],
        hbm,
    )(got, rel_grad, grad, *parts)
    return ent_grad.T, panel_grad, rel_grad


def solution(mesh):
    both = ("bucket", "entity")
    placed = (
        P("entity", None),
        P(both, None, None),
        P(both, None),
        P(both, None, None),
        P(both, None, None),
        P(both, None, None),
        P(both, None, None),
        P(both),
    )
    return jax.shard_map(
        body,
        mesh=mesh,
        in_specs=placed,
        out_specs=(P("entity", "bucket"), P(both, None, None), P(both, None)),
        check_vma=False,
    )
```

```python
import functools

import jax
import jax.numpy as jnp
from jax import lax
from jax.experimental import pallas as pl
from jax.experimental.pallas import tpu as pltpu
from jax.sharding import PartitionSpec as P

MARGIN = 2.0
LANES = 128
FOLD = 4
DIGIT = 256
F32 = jnp.float32
BF16 = jnp.bfloat16
I32 = jnp.int32
VMEM_BYTES = 16 * 1024 * 1024


def dot(a, b, over):
    return lax.dot_general(a, b, ((over[:1], over[1:]), ((), ())), preferred_element_type=F32)


def iota(shape, axis):
    return lax.broadcasted_iota(I32, shape, axis)


def to_column(row_blocks):
    k = row_blocks[0].shape[1]
    tall = jnp.concatenate([jnp.broadcast_to(r, (k, k)) for r in row_blocks], axis=0)
    pick = lax.rem(iota(tall.shape, 0), k) == iota(tall.shape, 1)
    return jnp.sum(jnp.where(pick, tall, 0).astype(F32), axis=1, keepdims=True)


def flip(column):
    n = column.shape[0]
    return jnp.sum(jnp.where(iota((n, n), 0) == iota((n, n), 1), column, 0.0), axis=0, keepdims=True)


def call(kernel, ins, outs, scratch=(), space=pltpu.VMEM):
    return pl.pallas_call(
        kernel,
        out_shape=outs,
        in_specs=[pl.BlockSpec(memory_space=place) for place in ins],
        out_specs=[pl.BlockSpec(memory_space=space)] * len(outs),
        scratch_shapes=list(scratch),
        compiler_params=pltpu.CompilerParams(vmem_limit_bytes=VMEM_BYTES),
    )


def prepare_kernel(
    count_ref, head_hbm, tail_hbm, neg_hbm, req_hbm, table_hbm, panel_hbm, rel_hbm,
    edges_ref, pairs_ref, rows_ref, req_ref, table_ref, panel_ref, rel_ref,
    head_ref, tail_ref, neg_ref, sems,
):
    moves = [
        pltpu.make_async_copy(src, dst, sems.at[i])
        for i, (src, dst) in enumerate(
            [
                (head_hbm, head_ref),
                (tail_hbm, tail_ref),
                (neg_hbm, neg_ref),
                (req_hbm, req_ref),
                (rel_hbm, rel_ref),
                (table_hbm, table_ref),
                (panel_hbm, panel_ref),
            ]
        )
    ]
    for move in moves:
        move.start()
    for move in moves[:4]:
        move.wait()
    shards, cap = req_ref.shape[1:]
    total = shards * cap
    me = lax.axis_index("entity")
    blocks, edge = head_ref.shape[1:]
    negs = neg_ref.shape[2]
    live_blocks = count_ref[0]
    edges = jnp.zeros((2 * total, 2 * total), F32)
    pairs = jnp.zeros((total, 2 * total), F32)
    left = iota(pairs.shape, 1) < total
    edge_slot = jnp.bitwise_xor(iota((total, edge), 0), me * cap)
    neg_slot = jnp.bitwise_xor(iota((total, negs), 0), me * cap)
    for j in range(blocks):
        live = (j < live_blocks).astype(F32)
        head = (head_ref[0, j : j + 1, :] == edge_slot).astype(F32) * live
        tail = (tail_ref[0, j : j + 1, :] == edge_slot).astype(F32)
        neg = (neg_ref[0, j : j + 1, :] == neg_slot).astype(F32)
        ends = jnp.concatenate([head, tail], axis=0).astype(BF16)
        edges += dot(ends, ends, (1, 1))
        heads = jnp.sum(head, axis=1, keepdims=True)
        others = jnp.sum(neg, axis=1, keepdims=True)
        pairs += jnp.where(left, others, heads) * flip(jnp.concatenate([heads, others], axis=0))
    edges_ref[...] = jnp.where(left, edges[total:], edges[:total])
    pairs_ref[...] = pairs
    numbers = jnp.concatenate([req_ref[0, pl.ds(jnp.bitwise_xor(me, s), 1), :] for s in range(shards)], axis=0)
    lane = iota((shards, LANES), 1)
    span = LANES // (cap // FOLD)
    for i in range(FOLD):
        spread = jnp.zeros((shards, LANES), I32)
        for k in range(cap // FOLD):
            spread = jnp.where(lane // span == k, numbers[:, k * FOLD + i : k * FOLD + i + 1], spread)
        digit = jnp.where(lane % span < span // 2, spread // DIGIT, spread % DIGIT)
        rows_ref[:, i, :] = digit.astype(F32)
    for move in moves[4:]:
        move.wait()


def pick_kernel(first, near_ref, other_ref, asked_ref, out_ref):
    me = lax.axis_index("entity")
    cap = asked_ref.shape[2]
    for k, table_ref in enumerate((near_ref, other_ref)):
        column = to_column([asked_ref[0, pl.ds(jnp.bitwise_xor(me, k), 1), :]]).astype(I32)
        hot = (column == iota((cap, table_ref.shape[0]), 1)).astype(F32).astype(BF16)
        at = (first ^ k) * cap
        out_ref[at : at + cap] = dot(hot, table_ref[...], (1, 0)).astype(BF16)


def turn_kernel(panel_ref, out_ref):
    out_ref[...] = jnp.transpose(panel_ref[0])


def terms_kernel(buckets, negs, *refs):
    panel_ref, turned_ref, rel_ref, edges_ref, pairs_ref, rows_ref = refs[:6]
    send_ref, grad_ref, rel_grad_ref = refs[-3:]
    fetched = jnp.concatenate([r[...] for r in refs[6:-3]], axis=0)
    proj = dot(fetched, turned_ref[...], (1, 0)).astype(BF16)
    proj_f = proj.astype(F32)
    centers = (proj_f + rel_ref[...].astype(F32)).astype(BF16)
    center_f = centers.astype(F32)
    total, features = proj.shape
    points = jnp.concatenate([centers, proj], axis=0)
    gram = dot(points, points, (1, 1))
    norms = jnp.concatenate(
        [jnp.sum(x * x, axis=1, keepdims=True) for x in (center_f, proj_f)], axis=0
    )
    left = iota((total, 2 * total), 1) < total
    dist = (
        jnp.where(left, norms[total:], norms[:total])
        + flip(norms)
        - 2.0 * jnp.where(left, gram[total:], gram[:total])
    )
    pos = edges_ref[...] * jax.nn.sigmoid(dist - MARGIN)
    neg = -jax.nn.sigmoid(MARGIN - dist) * (1.0 / negs)
    exact = pos + pairs_ref[...] * neg
    rounded = pos + pairs_ref[...] * neg.astype(BF16).astype(F32)
    high = rounded.astype(BF16)
    low = (rounded - high.astype(F32)).astype(BF16)
    mixed = dot(jnp.concatenate([high, low], axis=0), points, (1, 0))
    from_centers = jnp.sum(jnp.where(left, 0.0, exact), axis=1, keepdims=True) * center_f
    from_others = jnp.sum(jnp.where(left, exact, 0.0), axis=1, keepdims=True) * proj_f
    grad = (2.0 * (from_centers + from_others - mixed[:total] - mixed[total:])).astype(BF16)
    grad_ref[...] = grad
    grad_rows = dot(grad, panel_ref[0], (1, 0))
    devices, tiles, _, _ = send_ref.shape
    shards = devices // buckets
    tiles -= 1
    width = features // buckets
    me = lax.axis_index("entity")
    lane = iota((total, LANES), 1)
    rows = rows_ref[...].astype(BF16)
    for b in range(buckets):
        block, offset = divmod(b * width, LANES)
        piece = grad_rows[:, block * LANES : (block + 1) * LANES]
        near = pltpu.roll(piece, LANES - offset, 1) if offset else piece
        far = pltpu.roll(piece, (LANES + LANES // 2 - offset) % LANES, 1) if offset != LANES // 2 else piece
        far = pltpu.roll(far, total - FOLD, 0)
        piece = jnp.where(lane < LANES // 2, near, far).reshape(total // (2 * FOLD), 2 * FOLD, LANES)
        piece = piece[:, :FOLD].astype(BF16)
        for s in range(shards):
            to = b * shards + jnp.bitwise_xor(me, s)
            send_ref[to, :tiles] = piece[s * tiles : (s + 1) * tiles]
            send_ref[to, tiles] = rows[s]
    from_others = jnp.sum(jnp.where(left, rounded, 0.0), axis=1, keepdims=True) * proj_f
    rel_grad_ref[...] = 2.0 * jnp.sum(from_centers - from_others, axis=0, keepdims=True)


def finish_kernel(width, got_ref, rel_grad_ref, grad_ref, *refs):
    parts, (sums_hbm, panel_hbm, rel_hbm, out_ref, panel_ref, sems) = refs[:-6], refs[-6:]
    fetched = jnp.concatenate([r[...] for r in parts], axis=0)
    moves = [pltpu.make_async_copy(rel_grad_ref, rel_hbm, sems.at[0])]
    moves[0].start()
    features = fetched.shape[1]
    half = features // 2
    for i in range(2):
        at = pl.ds(i * half, half)
        panel_ref[at] = dot(grad_ref[:, i * half : (i + 1) * half], fetched, (0, 0))
        moves.append(pltpu.make_async_copy(panel_ref.at[at], panel_hbm.at[0, at], sems.at[1 + i]))
        moves[-1].start()
    devices, tiles, _, _ = got_ref.shape
    tiles -= 1
    rows = out_ref.shape[1]
    step = min(devices, 32)
    span = LANES // (2 * tiles)

    def part(i):
        got = got_ref[pl.ds(i * step, step)].astype(F32)
        turned = [jnp.transpose(got[:, k].reshape(step * FOLD, LANES)) for k in range(tiles + 1)]
        starts = [(t, at) for t in turned[:tiles] for at in (0, LANES // 2)]
        values = jnp.concatenate([t[at : at + width] for t, at in starts], axis=1).astype(BF16)
        digits = [turned[tiles][k * span // 2 : k * span // 2 + 1] for k in range(4 * tiles)]
        high, low = jnp.concatenate(digits[0::2], axis=1), jnp.concatenate(digits[1::2], axis=1)
        hot = (low.astype(I32) == iota((DIGIT, low.shape[1]), 0)).astype(F32).astype(BF16)
        kept = [values * (high == float(h)).astype(F32).astype(BF16) for h in range(rows // DIGIT)]
        return dot(jnp.concatenate(kept, axis=0), hot, (1, 1))

    def store(sums, add):
        for h in range(rows // DIGIT):
            piece = sums[h * width : (h + 1) * width]
            at = slice(h * DIGIT, (h + 1) * DIGIT)
            out_ref[:, at] = out_ref[:, at] + piece if add else piece

    store(part(0), False)
    if devices > step:

        def more(i, _):
            store(part(i), True)
            return 0

        lax.fori_loop(1, devices // step, more, 0)
    moves.append(pltpu.make_async_copy(out_ref, sums_hbm, sems.at[3]))
    moves[-1].start()
    for move in moves:
        move.wait()


def body(ent_table, panels, rel_vecs, head_slots, tail_slots, negatives, requests, block_count):
    shards = lax.axis_size("entity")
    buckets = lax.axis_size("bucket")
    shard_rows, features = ent_table.shape
    cap = requests.shape[2]
    total = shards * cap
    width = features // buckets

    def swap(x, s):
        return lax.ppermute(x, "entity", [(i, i ^ s) for i in range(shards)])

    def out(shape, dtype=F32):
        return jax.ShapeDtypeStruct(shape, dtype)

    def like(x):
        return out(x.shape, x.dtype)

    vmem, hbm = pltpu.VMEM, pltpu.HBM
    asked = [swap(requests, s) for s in range(3, shards, 2)]
    other = swap(ent_table, 1)
    edges, pairs, rows, own, table, panel, rel = call(
        prepare_kernel,
        [pltpu.SMEM] + [hbm] * 7,
        [out((total, 2 * total)), out((total, 2 * total)), out((shards, FOLD, LANES))]
        + [like(x) for x in (requests, ent_table, panels, rel_vecs)],
        [
            pltpu.VMEM(head_slots.shape, I32),
            pltpu.VMEM(tail_slots.shape, I32),
            pltpu.VMEM(negatives.shape, I32),
            pltpu.SemaphoreType.DMA((7,)),
        ],
    )(
        block_count,
        *[
            pltpu.with_memory_space_constraint(x, hbm)
            for x in (head_slots, tail_slots, negatives, requests, ent_table, panels, rel_vecs)
        ]
    )

    def pick(first, ids):
        kernel = functools.partial(pick_kernel, first)
        return call(kernel, [vmem] * 3, [out((2 * cap, features), BF16)])(table, other, ids)[0]

    found = [pick(1, ids) for ids in asked]
    parts = [pick(0, own)] + [swap(x, 2 * c + 3) for c, x in enumerate(found)]
    [turned] = call(turn_kernel, [vmem], [out((features, features), BF16)])(panel)
    send, grad, rel_grad = call(
        lambda *refs: terms_kernel(buckets, negatives.shape[2], *refs),
        [vmem] * (6 + len(parts)),
        [out((buckets * shards, cap // (2 * FOLD) + 1, FOLD, LANES), BF16), out((total, features), BF16), out((1, features))],
    )(panel, turned, rel, edges, pairs, rows, *parts)
    got = lax.all_to_all(send, ("bucket", "entity"), split_axis=0, concat_axis=0, tiled=True)
    ent_grad, panel_grad, rel_grad = call(
        functools.partial(finish_kernel, width),
        [vmem] * (3 + len(parts)),
        [out((width, shard_rows)), out((1, features, features)), out((1, features))],
        [
            pltpu.VMEM((width, shard_rows), F32),
            pltpu.VMEM((features, features), F32),
            pltpu.SemaphoreType.DMA((4,)),
        ],
        hbm,
    )(got, rel_grad, grad, *parts)
    return ent_grad.T, panel_grad, rel_grad


def solution(mesh):
    both = ("bucket", "entity")
    placed = (
        P("entity", None),
        P(both, None, None),
        P(both, None),
        P(both, None, None),
        P(both, None, None),
        P(both, None, None),
        P(both, None, None),
        P(both),
    )
    return jax.shard_map(
        body,
        mesh=mesh,
        in_specs=placed,
        out_specs=(P("entity", "bucket"), P(both, None, None), P(both, None)),
        check_vma=False,
    )
```

```python
import functools

import jax
import jax.numpy as jnp
from jax import lax
from jax.experimental import pallas as pl
from jax.experimental.pallas import tpu as pltpu
from jax.sharding import PartitionSpec as P

MARGIN = 2.0
LANES = 128
FOLD = 4
DIGIT = 256
F32 = jnp.float32
BF16 = jnp.bfloat16
I32 = jnp.int32
VMEM_BYTES = 16 * 1024 * 1024


def dot(a, b, over):
    return lax.dot_general(a, b, ((over[:1], over[1:]), ((), ())), preferred_element_type=F32)


def iota(shape, axis):
    return lax.broadcasted_iota(I32, shape, axis)


def to_column(row_blocks):
    k = row_blocks[0].shape[1]
    tall = jnp.concatenate([jnp.broadcast_to(r, (k, k)) for r in row_blocks], axis=0)
    pick = lax.rem(iota(tall.shape, 0), k) == iota(tall.shape, 1)
    return jnp.sum(jnp.where(pick, tall, 0).astype(F32), axis=1, keepdims=True)


def flip(column):
    n = column.shape[0]
    return jnp.sum(jnp.where(iota((n, n), 0) == iota((n, n), 1), column, 0.0), axis=0, keepdims=True)


def call(kernel, ins, outs, scratch=(), space=pltpu.VMEM):
    return pl.pallas_call(
        kernel,
        out_shape=outs,
        in_specs=[pl.BlockSpec(memory_space=place) for place in ins],
        out_specs=[pl.BlockSpec(memory_space=space)] * len(outs),
        scratch_shapes=list(scratch),
        compiler_params=pltpu.CompilerParams(vmem_limit_bytes=VMEM_BYTES),
    )


def prepare_kernel(
    count_ref, head_hbm, tail_hbm, neg_hbm, req_hbm, table_hbm, panel_hbm, rel_hbm,
    edges_ref, pairs_ref, rows_ref, req_ref, table_ref, panel_ref, rel_ref,
    head_ref, tail_ref, neg_ref, sems,
):
    moves = [
        pltpu.make_async_copy(src, dst, sems.at[i])
        for i, (src, dst) in enumerate(
            [
                (head_hbm, head_ref),
                (tail_hbm, tail_ref),
                (neg_hbm, neg_ref),
                (req_hbm, req_ref),
                (rel_hbm, rel_ref),
                (table_hbm, table_ref),
                (panel_hbm, panel_ref),
            ]
        )
    ]
    for move in moves:
        move.start()
    for move in moves[:4]:
        move.wait()
    shards, cap = req_ref.shape[1:]
    total = shards * cap
    me = lax.axis_index("entity")
    blocks, edge = head_ref.shape[1:]
    negs = neg_ref.shape[2]
    live_blocks = count_ref[0]
    edges = jnp.zeros((2 * total, 2 * total), F32)
    pairs = jnp.zeros((total, 2 * total), F32)
    left = iota(pairs.shape, 1) < total
    edge_slot = jnp.bitwise_xor(iota((total, edge), 0), me * cap)
    neg_slot = jnp.bitwise_xor(iota((total, negs), 0), me * cap)
    for j in range(blocks):
        live = (j < live_blocks).astype(F32)
        head = (head_ref[0, j : j + 1, :] == edge_slot).astype(F32) * live
        tail = (tail_ref[0, j : j + 1, :] == edge_slot).astype(F32)
        neg = (neg_ref[0, j : j + 1, :] == neg_slot).astype(F32)
        ends = jnp.concatenate([head, tail], axis=0).astype(BF16)
        edges += dot(ends, ends, (1, 1))
        heads = jnp.sum(head, axis=1, keepdims=True)
        others = jnp.sum(neg, axis=1, keepdims=True)
        pairs += jnp.where(left, others, heads) * flip(jnp.concatenate([heads, others], axis=0))
    edges_ref[...] = jnp.where(left, edges[total:], edges[:total])
    pairs_ref[...] = pairs
    numbers = jnp.concatenate([req_ref[0, pl.ds(jnp.bitwise_xor(me, s), 1), :] for s in range(shards)], axis=0)
    lane = iota((shards, LANES), 1)
    span = LANES // (cap // FOLD)
    for i in range(FOLD):
        spread = jnp.zeros((shards, LANES), I32)
        for k in range(cap // FOLD):
            spread = jnp.where(lane // span == k, numbers[:, k * FOLD + i : k * FOLD + i + 1], spread)
        digit = jnp.where(lane % span < span // 2, spread // DIGIT, spread % DIGIT)
        rows_ref[:, i, :] = digit.astype(F32)
    for move in moves[4:]:
        move.wait()


def pick_kernel(first, near_ref, other_ref, asked_ref, out_ref):
    me = lax.axis_index("entity")
    cap = asked_ref.shape[2]
    for k, table_ref in enumerate((near_ref, other_ref)):
        column = to_column([asked_ref[0, pl.ds(jnp.bitwise_xor(me, k), 1), :]]).astype(I32)
        hot = (column == iota((cap, table_ref.shape[0]), 1)).astype(F32).astype(BF16)
        at = (first ^ k) * cap
        out_ref[at : at + cap] = dot(hot, table_ref[...], (1, 0)).astype(BF16)


def turn_kernel(panel_ref, out_ref):
    out_ref[...] = jnp.transpose(panel_ref[0])


def terms_kernel(buckets, negs, *refs):
    panel_ref, turned_ref, rel_ref, edges_ref, pairs_ref, rows_ref = refs[:6]
    send_ref, panel_grad_ref, rel_grad_ref = refs[-3:]
    fetched = jnp.concatenate([r[...] for r in refs[6:-3]], axis=0)
    proj = dot(fetched, turned_ref[...], (1, 0)).astype(BF16)
    proj_f = proj.astype(F32)
    centers = (proj_f + rel_ref[...].astype(F32)).astype(BF16)
    center_f = centers.astype(F32)
    total, features = proj.shape
    points = jnp.concatenate([centers, proj], axis=0)
    gram = dot(points, points, (1, 1))
    norms = jnp.concatenate(
        [jnp.sum(x * x, axis=1, keepdims=True) for x in (center_f, proj_f)], axis=0
    )
    left = iota((total, 2 * total), 1) < total
    dist = (
        jnp.where(left, norms[total:], norms[:total])
        + flip(norms)
        - 2.0 * jnp.where(left, gram[total:], gram[:total])
    )
    pos = edges_ref[...] * jax.nn.sigmoid(dist - MARGIN)
    neg = -jax.nn.sigmoid(MARGIN - dist) * (1.0 / negs)
    exact = pos + pairs_ref[...] * neg
    rounded = pos + pairs_ref[...] * neg.astype(BF16).astype(F32)
    high = rounded.astype(BF16)
    low = (rounded - high.astype(F32)).astype(BF16)
    mixed = dot(jnp.concatenate([high, low], axis=0), points, (1, 0))
    from_centers = jnp.sum(jnp.where(left, 0.0, exact), axis=1, keepdims=True) * center_f
    from_others = jnp.sum(jnp.where(left, exact, 0.0), axis=1, keepdims=True) * proj_f
    grad = (2.0 * (from_centers + from_others - mixed[:total] - mixed[total:])).astype(BF16)
    grad_rows = dot(grad, panel_ref[0], (1, 0))
    panel_grad_ref[...] = dot(grad, fetched, (0, 0))
    devices, tiles, _, _ = send_ref.shape
    shards = devices // buckets
    tiles -= 1
    width = features // buckets
    me = lax.axis_index("entity")
    lane = iota((total, LANES), 1)
    rows = rows_ref[...].astype(BF16)
    for b in range(buckets):
        block, offset = divmod(b * width, LANES)
        piece = grad_rows[:, block * LANES : (block + 1) * LANES]
        near = pltpu.roll(piece, LANES - offset, 1) if offset else piece
        far = pltpu.roll(piece, (LANES + LANES // 2 - offset) % LANES, 1) if offset != LANES // 2 else piece
        far = pltpu.roll(far, total - FOLD, 0)
        piece = jnp.where(lane < LANES // 2, near, far).reshape(total // (2 * FOLD), 2 * FOLD, LANES)
        piece = piece[:, :FOLD].astype(BF16)
        for s in range(shards):
            to = b * shards + jnp.bitwise_xor(me, s)
            send_ref[to, :tiles] = piece[s * tiles : (s + 1) * tiles]
            send_ref[to, tiles] = rows[s]
    from_others = jnp.sum(jnp.where(left, rounded, 0.0), axis=1, keepdims=True) * proj_f
    rel_grad_ref[...] = 2.0 * jnp.sum(from_centers - from_others, axis=0, keepdims=True)


def finish_kernel(width, got_ref, panel_ref, rel_grad_ref, sums_hbm, panel_hbm, rel_hbm, out_ref, sems):
    moves = [
        pltpu.make_async_copy(panel_ref, panel_hbm.at[0], sems.at[0]),
        pltpu.make_async_copy(rel_grad_ref, rel_hbm, sems.at[1]),
    ]
    for move in moves:
        move.start()
    devices, tiles, _, _ = got_ref.shape
    tiles -= 1
    rows = out_ref.shape[1]
    step = min(devices, 32)
    span = LANES // (2 * tiles)

    def part(i):
        got = got_ref[pl.ds(i * step, step)].astype(F32)
        turned = [jnp.transpose(got[:, k].reshape(step * FOLD, LANES)) for k in range(tiles + 1)]
        starts = [(t, at) for t in turned[:tiles] for at in (0, LANES // 2)]
        values = jnp.concatenate([t[at : at + width] for t, at in starts], axis=1).astype(BF16)
        digits = [turned[tiles][k * span // 2 : k * span // 2 + 1] for k in range(4 * tiles)]
        high, low = jnp.concatenate(digits[0::2], axis=1), jnp.concatenate(digits[1::2], axis=1)
        hot = (low.astype(I32) == iota((DIGIT, low.shape[1]), 0)).astype(F32).astype(BF16)
        kept = [values * (high == float(h)).astype(F32).astype(BF16) for h in range(rows // DIGIT)]
        return dot(jnp.concatenate(kept, axis=0), hot, (1, 1))

    def store(sums, add):
        for h in range(rows // DIGIT):
            piece = sums[h * width : (h + 1) * width]
            at = slice(h * DIGIT, (h + 1) * DIGIT)
            out_ref[:, at] = out_ref[:, at] + piece if add else piece

    store(part(0), False)
    if devices > step:

        def more(i, _):
            store(part(i), True)
            return 0

        lax.fori_loop(1, devices // step, more, 0)
    moves.append(pltpu.make_async_copy(out_ref, sums_hbm, sems.at[2]))
    moves[-1].start()
    for move in moves:
        move.wait()


def body(ent_table, panels, rel_vecs, head_slots, tail_slots, negatives, requests, block_count):
    shards = lax.axis_size("entity")
    buckets = lax.axis_size("bucket")
    shard_rows, features = ent_table.shape
    cap = requests.shape[2]
    total = shards * cap
    width = features // buckets

    def swap(x, s):
        return lax.ppermute(x, "entity", [(i, i ^ s) for i in range(shards)])

    def out(shape, dtype=F32):
        return jax.ShapeDtypeStruct(shape, dtype)

    def like(x):
        return out(x.shape, x.dtype)

    vmem, hbm = pltpu.VMEM, pltpu.HBM
    asked = [swap(requests, s) for s in range(3, shards, 2)]
    other = swap(ent_table, 1)
    edges, pairs, rows, own, table, panel, rel = call(
        prepare_kernel,
        [pltpu.SMEM] + [hbm] * 7,
        [out((total, 2 * total)), out((total, 2 * total)), out((shards, FOLD, LANES))]
        + [like(x) for x in (requests, ent_table, panels, rel_vecs)],
        [
            pltpu.VMEM(head_slots.shape, I32),
            pltpu.VMEM(tail_slots.shape, I32),
            pltpu.VMEM(negatives.shape, I32),
            pltpu.SemaphoreType.DMA((7,)),
        ],
    )(
        block_count,
        *[
            pltpu.with_memory_space_constraint(x, hbm)
            for x in (head_slots, tail_slots, negatives, requests, ent_table, panels, rel_vecs)
        ]
    )

    def pick(first, ids):
        kernel = functools.partial(pick_kernel, first)
        return call(kernel, [vmem] * 3, [out((2 * cap, features), BF16)])(table, other, ids)[0]

    found = [pick(1, ids) for ids in asked]
    parts = [pick(0, own)] + [swap(x, 2 * c + 3) for c, x in enumerate(found)]
    [turned] = call(turn_kernel, [vmem], [out((features, features), BF16)])(panel)
    send, panel_grad, rel_grad = call(
        lambda *refs: terms_kernel(buckets, negatives.shape[2], *refs),
        [vmem] * (6 + len(parts)),
        [out((buckets * shards, cap // (2 * FOLD) + 1, FOLD, LANES), BF16), out((features, features)), out((1, features))],
    )(panel, turned, rel, edges, pairs, rows, *parts)
    got = lax.all_to_all(send, ("bucket", "entity"), split_axis=0, concat_axis=0, tiled=True)
    ent_grad, panel_grad, rel_grad = call(
        functools.partial(finish_kernel, width),
        [vmem] * 3,
        [out((width, shard_rows)), out((1, features, features)), out((1, features))],
        [
            pltpu.VMEM((width, shard_rows), F32),
            pltpu.SemaphoreType.DMA((3,)),
        ],
        hbm,
    )(got, panel_grad, rel_grad)
    return ent_grad.T, panel_grad, rel_grad


def solution(mesh):
    both = ("bucket", "entity")
    placed = (
        P("entity", None),
        P(both, None, None),
        P(both, None),
        P(both, None, None),
        P(both, None, None),
        P(both, None, None),
        P(both, None, None),
        P(both),
    )
    return jax.shard_map(
        body,
        mesh=mesh,
        in_specs=placed,
        out_specs=(P("entity", "bucket"), P(both, None, None), P(both, None)),
        check_vma=False,
    )
```

```python
import functools

import jax
import jax.numpy as jnp
from jax import lax
from jax.experimental import pallas as pl
from jax.experimental.pallas import tpu as pltpu
from jax.sharding import PartitionSpec as P

MARGIN = 2.0
LANES = 128
FOLD = 4
DIGIT = 256
F32 = jnp.float32
BF16 = jnp.bfloat16
I32 = jnp.int32
VMEM_BYTES = 16 * 1024 * 1024


def dot(a, b, over):
    return lax.dot_general(a, b, ((over[:1], over[1:]), ((), ())), preferred_element_type=F32)


def iota(shape, axis):
    return lax.broadcasted_iota(I32, shape, axis)


def to_column(row_blocks):
    k = row_blocks[0].shape[1]
    tall = jnp.concatenate([jnp.broadcast_to(r, (k, k)) for r in row_blocks], axis=0)
    pick = lax.rem(iota(tall.shape, 0), k) == iota(tall.shape, 1)
    return jnp.sum(jnp.where(pick, tall, 0).astype(F32), axis=1, keepdims=True)


def flip(column):
    n = column.shape[0]
    return jnp.sum(jnp.where(iota((n, n), 0) == iota((n, n), 1), column, 0.0), axis=0, keepdims=True)


def call(kernel, ins, outs, scratch=(), space=pltpu.VMEM):
    return pl.pallas_call(
        kernel,
        out_shape=outs,
        in_specs=[pl.BlockSpec(memory_space=place) for place in ins],
        out_specs=[pl.BlockSpec(memory_space=space)] * len(outs),
        scratch_shapes=list(scratch),
        compiler_params=pltpu.CompilerParams(vmem_limit_bytes=VMEM_BYTES),
    )


def prepare_kernel(
    count_ref, head_hbm, tail_hbm, neg_hbm, req_hbm, table_hbm, panel_hbm, rel_hbm,
    edges_ref, pairs_ref, rows_ref, req_ref, table_ref, panel_ref, rel_ref,
    head_ref, tail_ref, neg_ref, sems,
):
    moves = [
        pltpu.make_async_copy(src, dst, sems.at[i])
        for i, (src, dst) in enumerate(
            [
                (head_hbm, head_ref),
                (tail_hbm, tail_ref),
                (neg_hbm, neg_ref),
                (req_hbm, req_ref),
                (rel_hbm, rel_ref),
                (table_hbm, table_ref),
                (panel_hbm, panel_ref),
            ]
        )
    ]
    for move in moves:
        move.start()
    for move in moves[:4]:
        move.wait()
    shards, cap = req_ref.shape[1:]
    total = shards * cap
    me = lax.axis_index("entity")
    blocks, edge = head_ref.shape[1:]
    negs = neg_ref.shape[2]
    live_blocks = count_ref[0]
    edges = jnp.zeros((2 * total, 2 * total), F32)
    pairs = jnp.zeros((total, 2 * total), F32)
    left = iota(pairs.shape, 1) < total
    edge_slot = jnp.bitwise_xor(iota((total, edge), 0), me * cap)
    neg_slot = jnp.bitwise_xor(iota((total, negs), 0), me * cap)
    for j in range(blocks):
        live = (j < live_blocks).astype(F32)
        head = (head_ref[0, j : j + 1, :] == edge_slot).astype(F32) * live
        tail = (tail_ref[0, j : j + 1, :] == edge_slot).astype(F32)
        neg = (neg_ref[0, j : j + 1, :] == neg_slot).astype(F32)
        ends = jnp.concatenate([head, tail], axis=0).astype(BF16)
        edges += dot(ends, ends, (1, 1))
        heads = jnp.sum(head, axis=1, keepdims=True)
        others = jnp.sum(neg, axis=1, keepdims=True)
        pairs += jnp.where(left, others, heads) * flip(jnp.concatenate([heads, others], axis=0))
    edges_ref[...] = jnp.where(left, edges[total:], edges[:total])
    pairs_ref[...] = pairs
    numbers = jnp.concatenate([req_ref[0, pl.ds(jnp.bitwise_xor(me, s), 1), :] for s in range(shards)], axis=0)
    lane = iota((shards, LANES), 1)
    span = LANES // (cap // FOLD)
    for i in range(FOLD):
        spread = jnp.zeros((shards, LANES), I32)
        for k in range(cap // FOLD):
            spread = jnp.where(lane // span == k, numbers[:, k * FOLD + i : k * FOLD + i + 1], spread)
        digit = jnp.where(lane % span < span // 2, spread // DIGIT, spread % DIGIT)
        rows_ref[:, i, :] = digit.astype(F32)
    for move in moves[4:]:
        move.wait()


def pick_kernel(first, near_ref, other_ref, asked_ref, out_ref):
    me = lax.axis_index("entity")
    cap = asked_ref.shape[2]
    for k, table_ref in enumerate((near_ref, other_ref)):
        column = to_column([asked_ref[0, pl.ds(jnp.bitwise_xor(me, k), 1), :]]).astype(I32)
        hot = (column == iota((cap, table_ref.shape[0]), 1)).astype(F32).astype(BF16)
        at = (first ^ k) * cap
        out_ref[at : at + cap] = dot(hot, table_ref[...], (1, 0)).astype(BF16)


def turn_kernel(panel_ref, out_ref):
    out_ref[...] = jnp.transpose(panel_ref[0])


def terms_kernel(buckets, negs, place, *refs):
    panel_ref, turned_ref, rel_ref, edges_ref, pairs_ref, rows_ref = refs[:6]
    send_ref, panel_grad_ref, rel_grad_ref = refs[-3:]
    fetched = jnp.concatenate([r[...] for r in refs[6:-3]], axis=0)
    proj = dot(fetched, turned_ref[...], (1, 0)).astype(BF16)
    proj_f = proj.astype(F32)
    centers = (proj_f + rel_ref[...].astype(F32)).astype(BF16)
    center_f = centers.astype(F32)
    total, features = proj.shape
    points = jnp.concatenate([centers, proj], axis=0)
    gram = dot(points, points, (1, 1))
    norms = jnp.concatenate(
        [jnp.sum(x * x, axis=1, keepdims=True) for x in (center_f, proj_f)], axis=0
    )
    left = iota((total, 2 * total), 1) < total
    dist = (
        jnp.where(left, norms[total:], norms[:total])
        + flip(norms)
        - 2.0 * jnp.where(left, gram[total:], gram[:total])
    )
    pos = edges_ref[...] * jax.nn.sigmoid(dist - MARGIN)
    neg = -jax.nn.sigmoid(MARGIN - dist) * (1.0 / negs)
    exact = pos + pairs_ref[...] * neg
    rounded = pos + pairs_ref[...] * neg.astype(BF16).astype(F32)
    high = rounded.astype(BF16)
    low = (rounded - high.astype(F32)).astype(BF16)
    mixed = dot(jnp.concatenate([high, low], axis=0), points, (1, 0))
    from_centers = jnp.sum(jnp.where(left, 0.0, exact), axis=1, keepdims=True) * center_f
    from_others = jnp.sum(jnp.where(left, exact, 0.0), axis=1, keepdims=True) * proj_f
    grad = (2.0 * (from_centers + from_others - mixed[:total] - mixed[total:])).astype(BF16)
    grad_rows = dot(grad, panel_ref[0], (1, 0))
    panel_grad_ref[...] = dot(grad, fetched, (0, 0))
    devices, tiles, _, _ = send_ref.shape
    shards = devices // buckets
    tiles -= 1
    width = features // buckets
    me = lax.axis_index("entity")
    lane = iota((total, LANES), 1)
    rows = rows_ref[...].astype(BF16)
    for b in range(buckets):
        block, offset = divmod(b * width, LANES)
        piece = grad_rows[:, block * LANES : (block + 1) * LANES]
        near = pltpu.roll(piece, LANES - offset, 1) if offset else piece
        far = pltpu.roll(piece, (LANES + LANES // 2 - offset) % LANES, 1) if offset != LANES // 2 else piece
        far = pltpu.roll(far, total - FOLD, 0)
        piece = jnp.where(lane < LANES // 2, near, far).reshape(total // (2 * FOLD), 2 * FOLD, LANES)
        piece = piece[:, :FOLD].astype(BF16)
        for s in range(shards):
            to = lax.rem((b * shards + jnp.bitwise_xor(me, s)) * place, devices)
            send_ref[to, :tiles] = piece[s * tiles : (s + 1) * tiles]
            send_ref[to, tiles] = rows[s]
    from_others = jnp.sum(jnp.where(left, rounded, 0.0), axis=1, keepdims=True) * proj_f
    rel_grad_ref[...] = 2.0 * jnp.sum(from_centers - from_others, axis=0, keepdims=True)


def finish_kernel(width, got_ref, panel_ref, rel_grad_ref, sums_hbm, panel_hbm, rel_hbm, out_ref, sems):
    moves = [
        pltpu.make_async_copy(panel_ref, panel_hbm.at[0], sems.at[0]),
        pltpu.make_async_copy(rel_grad_ref, rel_hbm, sems.at[1]),
    ]
    for move in moves:
        move.start()
    devices, tiles, _, _ = got_ref.shape
    tiles -= 1
    rows = out_ref.shape[1]
    step = min(devices, 32)
    span = LANES // (2 * tiles)

    def part(i):
        got = got_ref[pl.ds(i * step, step)].astype(F32)
        flat = [got[:, k].reshape(step * FOLD, LANES) for k in range(tiles + 1)]
        group = max(1, LANES // (step * FOLD))
        turned = [jnp.transpose(jnp.concatenate(flat[k : k + group], axis=0)) for k in range(0, tiles, group)]
        values = [t[at : at + width] for t in turned for at in (0, LANES // 2)]
        values = jnp.concatenate(values, axis=1).astype(BF16)
        digits = jnp.transpose(flat[tiles])
        places = [2 * (k + g) + half for k in range(0, tiles, group) for half in (0, 1) for g in range(group)]
        high = jnp.concatenate([digits[p * span : p * span + 1] for p in places], axis=1)
        low = jnp.concatenate([digits[p * span + span // 2 : p * span + span // 2 + 1] for p in places], axis=1)
        hot = (low.astype(I32) == iota((DIGIT, low.shape[1]), 0)).astype(F32).astype(BF16)
        kept = [values * (high == float(h)).astype(F32).astype(BF16) for h in range(rows // DIGIT)]
        return dot(jnp.concatenate(kept, axis=0), hot, (1, 1))

    def store(sums, add):
        for h in range(rows // DIGIT):
            piece = sums[h * width : (h + 1) * width]
            at = slice(h * DIGIT, (h + 1) * DIGIT)
            out_ref[:, at] = out_ref[:, at] + piece if add else piece

    store(part(0), False)
    if devices > step:

        def more(i, _):
            store(part(i), True)
            return 0

        lax.fori_loop(1, devices // step, more, 0)
    moves.append(pltpu.make_async_copy(out_ref, sums_hbm, sems.at[2]))
    moves[-1].start()
    for move in moves:
        move.wait()


def body(ent_table, panels, rel_vecs, head_slots, tail_slots, negatives, requests, block_count):
    shards = lax.axis_size("entity")
    buckets = lax.axis_size("bucket")
    shard_rows, features = ent_table.shape
    cap = requests.shape[2]
    total = shards * cap
    width = features // buckets

    def swap(x, s):
        return lax.ppermute(x, "entity", [(i, i ^ s) for i in range(shards)])

    def out(shape, dtype=F32):
        return jax.ShapeDtypeStruct(shape, dtype)

    def like(x):
        return out(x.shape, x.dtype)

    vmem, hbm = pltpu.VMEM, pltpu.HBM
    asked = [swap(requests, s) for s in range(3, shards, 2)]
    other = swap(ent_table, 1)
    edges, pairs, rows, own, table, panel, rel = call(
        prepare_kernel,
        [pltpu.SMEM] + [hbm] * 7,
        [out((total, 2 * total)), out((total, 2 * total)), out((shards, FOLD, LANES))]
        + [like(x) for x in (requests, ent_table, panels, rel_vecs)],
        [
            pltpu.VMEM(head_slots.shape, I32),
            pltpu.VMEM(tail_slots.shape, I32),
            pltpu.VMEM(negatives.shape, I32),
            pltpu.SemaphoreType.DMA((7,)),
        ],
    )(
        block_count,
        *[
            pltpu.with_memory_space_constraint(x, hbm)
            for x in (head_slots, tail_slots, negatives, requests, ent_table, panels, rel_vecs)
        ]
    )

    def pick(first, ids):
        kernel = functools.partial(pick_kernel, first)
        return call(kernel, [vmem] * 3, [out((2 * cap, features), BF16)])(table, other, ids)[0]

    found = [pick(1, ids) for ids in asked]
    parts = [pick(0, own)] + [swap(x, 2 * c + 3) for c, x in enumerate(found)]
    devices = buckets * shards
    stride = devices - 5
    order = [p * stride % devices for p in range(devices)]
    [turned] = call(turn_kernel, [vmem], [out((features, features), BF16)])(panel)
    send, panel_grad, rel_grad = call(
        functools.partial(terms_kernel, buckets, negatives.shape[2], pow(stride, -1, devices)),
        [vmem] * (6 + len(parts)),
        [out((devices, cap // (2 * FOLD) + 1, FOLD, LANES), BF16), out((features, features)), out((1, features))],
    )(panel, turned, rel, edges, pairs, rows, *parts)
    got = lax.all_to_all(
        send, ("bucket", "entity"), split_axis=0, concat_axis=0, tiled=True, axis_index_groups=[order]
    )
    ent_grad, panel_grad, rel_grad = call(
        functools.partial(finish_kernel, width),
        [vmem] * 3,
        [out((width, shard_rows)), out((1, features, features)), out((1, features))],
        [
            pltpu.VMEM((width, shard_rows), F32),
            pltpu.SemaphoreType.DMA((3,)),
        ],
        hbm,
    )(got, panel_grad, rel_grad)
    return ent_grad.T, panel_grad, rel_grad


def solution(mesh):
    both = ("bucket", "entity")
    placed = (
        P("entity", None),
        P(both, None, None),
        P(both, None),
        P(both, None, None),
        P(both, None, None),
        P(both, None, None),
        P(both, None, None),
        P(both),
    )
    return jax.shard_map(
        body,
        mesh=mesh,
        in_specs=placed,
        out_specs=(P("entity", "bucket"), P(both, None, None), P(both, None)),
        check_vma=False,
    )
```

```python
import functools

import jax
import jax.numpy as jnp
from jax import lax
from jax.experimental import pallas as pl
from jax.experimental.pallas import tpu as pltpu
from jax.sharding import PartitionSpec as P

MARGIN = 2.0
LANES = 128
FOLD = 4
DIGIT = 256
F32 = jnp.float32
BF16 = jnp.bfloat16
I32 = jnp.int32
VMEM_BYTES = 16 * 1024 * 1024


def dot(a, b, over):
    return lax.dot_general(a, b, ((over[:1], over[1:]), ((), ())), preferred_element_type=F32)


def iota(shape, axis):
    return lax.broadcasted_iota(I32, shape, axis)


def flip(column):
    n = column.shape[0]
    return jnp.sum(jnp.where(iota((n, n), 0) == iota((n, n), 1), column, 0.0), axis=0, keepdims=True)


def call(kernel, ins, outs, scratch=(), space=pltpu.VMEM):
    return pl.pallas_call(
        kernel,
        out_shape=outs,
        in_specs=[pl.BlockSpec(memory_space=place) for place in ins],
        out_specs=[pl.BlockSpec(memory_space=space)] * len(outs),
        scratch_shapes=list(scratch),
        compiler_params=pltpu.CompilerParams(vmem_limit_bytes=VMEM_BYTES),
    )


def prepare_kernel(
    count_ref, head_hbm, tail_hbm, neg_hbm, req_hbm, table_hbm, panel_hbm, rel_hbm,
    edges_ref, pairs_ref, rows_ref, req_ref, table_ref, panel_ref, rel_ref,
    head_ref, tail_ref, neg_ref, sems,
):
    moves = [
        pltpu.make_async_copy(src, dst, sems.at[i])
        for i, (src, dst) in enumerate(
            [
                (head_hbm, head_ref),
                (tail_hbm, tail_ref),
                (neg_hbm, neg_ref),
                (req_hbm, req_ref),
                (rel_hbm, rel_ref),
                (table_hbm, table_ref),
                (panel_hbm, panel_ref),
            ]
        )
    ]
    for move in moves:
        move.start()
    for move in moves[:4]:
        move.wait()
    shards, cap = req_ref.shape[1:]
    total = shards * cap
    me = lax.axis_index("entity")
    blocks, edge = head_ref.shape[1:]
    negs = neg_ref.shape[2]
    live_blocks = count_ref[0]
    edges = jnp.zeros((2 * total, 2 * total), F32)
    pairs = jnp.zeros((total, 2 * total), F32)
    left = iota(pairs.shape, 1) < total
    edge_slot = jnp.bitwise_xor(iota((total, edge), 0), me * cap)
    neg_slot = jnp.bitwise_xor(iota((total, negs), 0), me * cap)
    for j in range(blocks):
        live = (j < live_blocks).astype(F32)
        head = (head_ref[0, j : j + 1, :] == edge_slot).astype(F32) * live
        tail = (tail_ref[0, j : j + 1, :] == edge_slot).astype(F32)
        neg = (neg_ref[0, j : j + 1, :] == neg_slot).astype(F32)
        ends = jnp.concatenate([head, tail], axis=0).astype(BF16)
        edges += dot(ends, ends, (1, 1))
        heads = jnp.sum(head, axis=1, keepdims=True)
        others = jnp.sum(neg, axis=1, keepdims=True)
        pairs += jnp.where(left, others, heads) * flip(jnp.concatenate([heads, others], axis=0))
    edges_ref[...] = jnp.where(left, edges[total:], edges[:total])
    pairs_ref[...] = pairs
    numbers = jnp.concatenate([req_ref[0, pl.ds(jnp.bitwise_xor(me, s), 1), :] for s in range(shards)], axis=0)
    lane = iota((shards, LANES), 1)
    span = LANES // (cap // FOLD)
    for i in range(FOLD):
        spread = jnp.zeros((shards, LANES), I32)
        for k in range(cap // FOLD):
            spread = jnp.where(lane // span == k, numbers[:, k * FOLD + i : k * FOLD + i + 1], spread)
        digit = jnp.where(lane % span < span // 2, spread // DIGIT, spread % DIGIT)
        rows_ref[:, i, :] = digit.astype(F32)
    for move in moves[4:]:
        move.wait()


def pick_kernel(first, near_ref, other_ref, asked_ref, out_ref):
    me = lax.axis_index("entity")
    cap = asked_ref.shape[2]
    for k, table_ref in enumerate((near_ref, other_ref)):
        asked = asked_ref[0, pl.ds(jnp.bitwise_xor(me, k), 1), :]
        hot = (asked == iota((table_ref.shape[0], cap), 0)).astype(F32).astype(BF16)
        at = (first ^ k) * cap
        out_ref[at : at + cap] = dot(hot, table_ref[...], (0, 0)).astype(BF16)


def turn_kernel(panel_ref, out_ref):
    out_ref[...] = jnp.transpose(panel_ref[0])


def terms_kernel(buckets, negs, place, *refs):
    panel_ref, turned_ref, rel_ref, edges_ref, pairs_ref, rows_ref = refs[:6]
    send_ref, panel_grad_ref, rel_grad_ref = refs[-3:]
    fetched = jnp.concatenate([r[...] for r in refs[6:-3]], axis=0)
    proj = dot(fetched, turned_ref[...], (1, 0)).astype(BF16)
    proj_f = proj.astype(F32)
    centers = (proj_f + rel_ref[...].astype(F32)).astype(BF16)
    center_f = centers.astype(F32)
    total, features = proj.shape
    points = jnp.concatenate([centers, proj], axis=0)
    gram = dot(points, points, (1, 1))
    norms = jnp.concatenate(
        [jnp.sum(x * x, axis=1, keepdims=True) for x in (center_f, proj_f)], axis=0
    )
    left = iota((total, 2 * total), 1) < total
    dist = (
        jnp.where(left, norms[total:], norms[:total])
        + flip(norms)
        - 2.0 * jnp.where(left, gram[total:], gram[:total])
    )
    pos = edges_ref[...] * jax.nn.sigmoid(dist - MARGIN)
    neg = -jax.nn.sigmoid(MARGIN - dist) * (1.0 / negs)
    exact = pos + pairs_ref[...] * neg
    rounded = pos + pairs_ref[...] * neg.astype(BF16).astype(F32)
    high = rounded.astype(BF16)
    low = (rounded - high.astype(F32)).astype(BF16)
    mixed = dot(jnp.concatenate([high, low], axis=0), points, (1, 0))
    from_centers = jnp.sum(jnp.where(left, 0.0, exact), axis=1, keepdims=True) * center_f
    from_others = jnp.sum(jnp.where(left, exact, 0.0), axis=1, keepdims=True) * proj_f
    grad = (2.0 * (from_centers + from_others - mixed[:total] - mixed[total:])).astype(BF16)
    grad_rows = dot(grad, panel_ref[0], (1, 0))
    panel_grad_ref[...] = dot(grad, fetched, (0, 0))
    devices, tiles, _, _ = send_ref.shape
    shards = devices // buckets
    tiles -= 1
    width = features // buckets
    me = lax.axis_index("entity")
    lane = iota((total, LANES), 1)
    rows = rows_ref[...].astype(BF16)
    for b in range(buckets):
        block, offset = divmod(b * width, LANES)
        piece = grad_rows[:, block * LANES : (block + 1) * LANES]
        near = pltpu.roll(piece, LANES - offset, 1) if offset else piece
        far = pltpu.roll(piece, (LANES + LANES // 2 - offset) % LANES, 1) if offset != LANES // 2 else piece
        far = pltpu.roll(far, total - FOLD, 0)
        piece = jnp.where(lane < LANES // 2, near, far).reshape(total // (2 * FOLD), 2 * FOLD, LANES)
        piece = piece[:, :FOLD].astype(BF16)
        for s in range(shards):
            to = lax.rem((b * shards + jnp.bitwise_xor(me, s)) * place, devices)
            send_ref[to, :tiles] = piece[s * tiles : (s + 1) * tiles]
            send_ref[to, tiles] = rows[s]
    from_others = jnp.sum(jnp.where(left, rounded, 0.0), axis=1, keepdims=True) * proj_f
    rel_grad_ref[...] = 2.0 * jnp.sum(from_centers - from_others, axis=0, keepdims=True)


def finish_kernel(width, got_ref, panel_ref, rel_grad_ref, sums_hbm, panel_hbm, rel_hbm, out_ref, sems):
    moves = [
        pltpu.make_async_copy(panel_ref, panel_hbm.at[0], sems.at[0]),
        pltpu.make_async_copy(rel_grad_ref, rel_hbm, sems.at[1]),
    ]
    for move in moves:
        move.start()
    devices, tiles, _, _ = got_ref.shape
    tiles -= 1
    rows = out_ref.shape[1]
    step = min(devices, 32)
    span = LANES // (2 * tiles)

    def part(i):
        got = got_ref[pl.ds(i * step, step)].astype(F32)
        flat = [got[:, k].reshape(step * FOLD, LANES) for k in range(tiles + 1)]
        group = max(1, LANES // (step * FOLD))
        turned = [jnp.transpose(jnp.concatenate(flat[k : k + group], axis=0)) for k in range(0, tiles, group)]
        values = [t[at : at + width] for t in turned for at in (0, LANES // 2)]
        values = jnp.concatenate(values, axis=1).astype(BF16)
        digits = jnp.transpose(flat[tiles])
        places = [2 * (k + g) + half for k in range(0, tiles, group) for half in (0, 1) for g in range(group)]
        high = jnp.concatenate([digits[p * span : p * span + 1] for p in places], axis=1)
        low = jnp.concatenate([digits[p * span + span // 2 : p * span + span // 2 + 1] for p in places], axis=1)
        hot = (low.astype(I32) == iota((DIGIT, low.shape[1]), 0)).astype(F32).astype(BF16)
        kept = [values * (high == float(h)).astype(F32).astype(BF16) for h in range(rows // DIGIT)]
        return dot(jnp.concatenate(kept, axis=0), hot, (1, 1))

    def store(sums, add):
        for h in range(rows // DIGIT):
            piece = sums[h * width : (h + 1) * width]
            at = slice(h * DIGIT, (h + 1) * DIGIT)
            out_ref[:, at] = out_ref[:, at] + piece if add else piece

    store(part(0), False)
    if devices > step:

        def more(i, _):
            store(part(i), True)
            return 0

        lax.fori_loop(1, devices // step, more, 0)
    moves.append(pltpu.make_async_copy(out_ref, sums_hbm, sems.at[2]))
    moves[-1].start()
    for move in moves:
        move.wait()


def body(ent_table, panels, rel_vecs, head_slots, tail_slots, negatives, requests, block_count):
    shards = lax.axis_size("entity")
    buckets = lax.axis_size("bucket")
    shard_rows, features = ent_table.shape
    cap = requests.shape[2]
    total = shards * cap
    width = features // buckets

    def swap(x, s):
        return lax.ppermute(x, "entity", [(i, i ^ s) for i in range(shards)])

    def out(shape, dtype=F32):
        return jax.ShapeDtypeStruct(shape, dtype)

    def like(x):
        return out(x.shape, x.dtype)

    vmem, hbm = pltpu.VMEM, pltpu.HBM
    asked = [swap(requests, s) for s in range(3, shards, 2)]
    other = swap(ent_table, 1)
    edges, pairs, rows, own, table, panel, rel = call(
        prepare_kernel,
        [pltpu.SMEM] + [hbm] * 7,
        [out((total, 2 * total)), out((total, 2 * total)), out((shards, FOLD, LANES))]
        + [like(x) for x in (requests, ent_table, panels, rel_vecs)],
        [
            pltpu.VMEM(head_slots.shape, I32),
            pltpu.VMEM(tail_slots.shape, I32),
            pltpu.VMEM(negatives.shape, I32),
            pltpu.SemaphoreType.DMA((7,)),
        ],
    )(
        block_count,
        *[
            pltpu.with_memory_space_constraint(x, hbm)
            for x in (head_slots, tail_slots, negatives, requests, ent_table, panels, rel_vecs)
        ]
    )

    def pick(first, ids):
        kernel = functools.partial(pick_kernel, first)
        return call(kernel, [vmem] * 3, [out((2 * cap, features), BF16)])(table, other, ids)[0]

    found = [pick(1, ids) for ids in asked]
    parts = [pick(0, own)] + [swap(x, 2 * c + 3) for c, x in enumerate(found)]
    devices = buckets * shards
    stride = devices - 5
    order = [p * stride % devices for p in range(devices)]
    [turned] = call(turn_kernel, [vmem], [out((features, features), BF16)])(panel)
    send, panel_grad, rel_grad = call(
        functools.partial(terms_kernel, buckets, negatives.shape[2], pow(stride, -1, devices)),
        [vmem] * (6 + len(parts)),
        [out((devices, cap // (2 * FOLD) + 1, FOLD, LANES), BF16), out((features, features)), out((1, features))],
    )(panel, turned, rel, edges, pairs, rows, *parts)
    got = lax.all_to_all(
        send, ("bucket", "entity"), split_axis=0, concat_axis=0, tiled=True, axis_index_groups=[order]
    )
    ent_grad, panel_grad, rel_grad = call(
        functools.partial(finish_kernel, width),
        [vmem] * 3,
        [out((width, shard_rows)), out((1, features, features)), out((1, features))],
        [
            pltpu.VMEM((width, shard_rows), F32),
            pltpu.SemaphoreType.DMA((3,)),
        ],
        hbm,
    )(got, panel_grad, rel_grad)
    return ent_grad.T, panel_grad, rel_grad


def solution(mesh):
    both = ("bucket", "entity")
    placed = (
        P("entity", None),
        P(both, None, None),
        P(both, None),
        P(both, None, None),
        P(both, None, None),
        P(both, None, None),
        P(both, None, None),
        P(both),
    )
    return jax.shard_map(
        body,
        mesh=mesh,
        in_specs=placed,
        out_specs=(P("entity", "bucket"), P(both, None, None), P(both, None)),
        check_vma=False,
    )
```

```python
import functools

import jax
import jax.numpy as jnp
from jax import lax
from jax.experimental import pallas as pl
from jax.experimental.pallas import tpu as pltpu
from jax.sharding import PartitionSpec as P

MARGIN = 2.0
LANES = 128
FOLD = 4
DIGIT = 256
F32 = jnp.float32
BF16 = jnp.bfloat16
I32 = jnp.int32
VMEM_BYTES = 16 * 1024 * 1024


def dot(a, b, over):
    return lax.dot_general(a, b, ((over[:1], over[1:]), ((), ())), preferred_element_type=F32)


def iota(shape, axis):
    return lax.broadcasted_iota(I32, shape, axis)


def flip(column):
    n = column.shape[0]
    return jnp.sum(jnp.where(iota((n, n), 0) == iota((n, n), 1), column, 0.0), axis=0, keepdims=True)


def call(kernel, ins, outs, scratch=(), space=pltpu.VMEM):
    return pl.pallas_call(
        kernel,
        out_shape=outs,
        in_specs=[pl.BlockSpec(memory_space=place) for place in ins],
        out_specs=[pl.BlockSpec(memory_space=space)] * len(outs),
        scratch_shapes=list(scratch),
        compiler_params=pltpu.CompilerParams(vmem_limit_bytes=VMEM_BYTES),
    )


def prepare_kernel(
    count_ref, head_hbm, tail_hbm, neg_hbm, req_hbm, table_hbm, panel_hbm, rel_hbm,
    edges_ref, pairs_ref, rows_ref, req_ref, table_ref, panel_ref, rel_ref,
    head_ref, tail_ref, neg_ref, sems,
):
    moves = [
        pltpu.make_async_copy(src, dst, sems.at[i])
        for i, (src, dst) in enumerate(
            [
                (head_hbm, head_ref),
                (tail_hbm, tail_ref),
                (neg_hbm, neg_ref),
                (req_hbm, req_ref),
                (rel_hbm, rel_ref),
                (table_hbm, table_ref),
                (panel_hbm, panel_ref),
            ]
        )
    ]
    for move in moves:
        move.start()
    for move in moves[:4]:
        move.wait()
    shards, cap = req_ref.shape[1:]
    total = shards * cap
    me = lax.axis_index("entity")
    blocks, edge = head_ref.shape[1:]
    negs = neg_ref.shape[2]
    live_blocks = count_ref[0]
    edges = jnp.zeros((2 * total, 2 * total), F32)
    pairs = jnp.zeros((total, 2 * total), F32)
    left = iota(pairs.shape, 1) < total
    edge_slot = jnp.bitwise_xor(iota((total, edge), 0), me * cap)
    neg_slot = jnp.bitwise_xor(iota((total, negs), 0), me * cap)
    for j in range(blocks):
        live = (j < live_blocks).astype(F32)
        head = (head_ref[0, j : j + 1, :] == edge_slot).astype(F32) * live
        tail = (tail_ref[0, j : j + 1, :] == edge_slot).astype(F32)
        neg = (neg_ref[0, j : j + 1, :] == neg_slot).astype(F32)
        ends = jnp.concatenate([head, tail], axis=0).astype(BF16)
        edges += dot(ends, ends, (1, 1))
        heads = jnp.sum(head, axis=1, keepdims=True)
        others = jnp.sum(neg, axis=1, keepdims=True)
        pairs += jnp.where(left, others, heads) * flip(jnp.concatenate([heads, others], axis=0))
    edges_ref[...] = jnp.where(left, edges[total:], edges[:total])
    pairs_ref[...] = pairs
    numbers = jnp.concatenate([req_ref[0, pl.ds(jnp.bitwise_xor(me, s), 1), :] for s in range(shards)], axis=0)
    lane = iota((shards, LANES), 1)
    span = LANES // (cap // FOLD)
    for i in range(FOLD):
        spread = jnp.zeros((shards, LANES), I32)
        for k in range(cap // FOLD):
            spread = jnp.where(lane // span == k, numbers[:, k * FOLD + i : k * FOLD + i + 1], spread)
        digit = jnp.where(lane % span < span // 2, spread // DIGIT, spread % DIGIT)
        rows_ref[:, i, :] = digit.astype(F32)
    for move in moves[4:]:
        move.wait()


def pick_kernel(first, near_ref, other_ref, asked_ref, out_ref):
    me = lax.axis_index("entity")
    cap = asked_ref.shape[2]
    for k, table_ref in enumerate((near_ref, other_ref)):
        asked = asked_ref[0, pl.ds(jnp.bitwise_xor(me, k), 1), :]
        hot = (asked == iota((table_ref.shape[0], cap), 0)).astype(F32).astype(BF16)
        at = (first ^ k) * cap
        out_ref[at : at + cap] = dot(hot, table_ref[...], (0, 0)).astype(BF16)


def project(rows, turned, relation):
    proj = dot(rows, turned, (1, 0)).astype(BF16)
    return (proj.astype(F32) + relation.astype(F32)).astype(BF16), proj


def near_kernel(panel_ref, rel_ref, rows_ref, turned_ref, centers_ref, proj_ref):
    turned_ref[...] = jnp.transpose(panel_ref[0])
    centers_ref[...], proj_ref[...] = project(rows_ref[...], turned_ref[...], rel_ref[...])


def terms_kernel(buckets, negs, place, *refs):
    panel_ref, turned_ref, rel_ref, edges_ref, pairs_ref, rows_ref, near_centers, near_proj = refs[:8]
    send_ref, panel_grad_ref, rel_grad_ref = refs[-3:]
    parts = refs[8:-3]
    fetched = jnp.concatenate([r[...] for r in parts], axis=0)
    far_centers, far_proj = project(fetched[near_proj.shape[0] :], turned_ref[...], rel_ref[...])
    proj = jnp.concatenate([near_proj[...], far_proj], axis=0)
    centers = jnp.concatenate([near_centers[...], far_centers], axis=0)
    proj_f = proj.astype(F32)
    center_f = centers.astype(F32)
    total, features = proj.shape
    points = jnp.concatenate([centers, proj], axis=0)
    gram = dot(points, points, (1, 1))
    norms = jnp.concatenate(
        [jnp.sum(x * x, axis=1, keepdims=True) for x in (center_f, proj_f)], axis=0
    )
    left = iota((total, 2 * total), 1) < total
    dist = (
        jnp.where(left, norms[total:], norms[:total])
        + flip(norms)
        - 2.0 * jnp.where(left, gram[total:], gram[:total])
    )
    pos = edges_ref[...] * jax.nn.sigmoid(dist - MARGIN)
    neg = -jax.nn.sigmoid(MARGIN - dist) * (1.0 / negs)
    exact = pos + pairs_ref[...] * neg
    rounded = pos + pairs_ref[...] * neg.astype(BF16).astype(F32)
    high = rounded.astype(BF16)
    low = (rounded - high.astype(F32)).astype(BF16)
    mixed = dot(jnp.concatenate([high, low], axis=0), points, (1, 0))
    from_centers = jnp.sum(jnp.where(left, 0.0, exact), axis=1, keepdims=True) * center_f
    from_others = jnp.sum(jnp.where(left, exact, 0.0), axis=1, keepdims=True) * proj_f
    grad = (2.0 * (from_centers + from_others - mixed[:total] - mixed[total:])).astype(BF16)
    grad_rows = dot(grad, panel_ref[0], (1, 0))
    panel_grad_ref[...] = dot(grad, fetched, (0, 0))
    devices, tiles, _, _ = send_ref.shape
    shards = devices // buckets
    tiles -= 1
    width = features // buckets
    me = lax.axis_index("entity")
    lane = iota((total, LANES), 1)
    rows = rows_ref[...].astype(BF16)
    for b in range(buckets):
        block, offset = divmod(b * width, LANES)
        piece = grad_rows[:, block * LANES : (block + 1) * LANES]
        near = pltpu.roll(piece, LANES - offset, 1) if offset else piece
        far = pltpu.roll(piece, (LANES + LANES // 2 - offset) % LANES, 1) if offset != LANES // 2 else piece
        far = pltpu.roll(far, total - FOLD, 0)
        piece = jnp.where(lane < LANES // 2, near, far).reshape(total // (2 * FOLD), 2 * FOLD, LANES)
        piece = piece[:, :FOLD].astype(BF16)
        for s in range(shards):
            to = lax.rem((b * shards + jnp.bitwise_xor(me, s)) * place, devices)
            send_ref[to, :tiles] = piece[s * tiles : (s + 1) * tiles]
            send_ref[to, tiles] = rows[s]
    from_others = jnp.sum(jnp.where(left, rounded, 0.0), axis=1, keepdims=True) * proj_f
    rel_grad_ref[...] = 2.0 * jnp.sum(from_centers - from_others, axis=0, keepdims=True)


def finish_kernel(width, got_ref, panel_ref, rel_grad_ref, sums_hbm, panel_hbm, rel_hbm, out_ref, sems):
    moves = [
        pltpu.make_async_copy(panel_ref, panel_hbm.at[0], sems.at[0]),
        pltpu.make_async_copy(rel_grad_ref, rel_hbm, sems.at[1]),
    ]
    for move in moves:
        move.start()
    devices, tiles, _, _ = got_ref.shape
    tiles -= 1
    rows = out_ref.shape[1]
    step = min(devices, 32)
    span = LANES // (2 * tiles)

    def part(i):
        got = got_ref[pl.ds(i * step, step)].astype(F32)
        flat = [got[:, k].reshape(step * FOLD, LANES) for k in range(tiles + 1)]
        group = max(1, LANES // (step * FOLD))
        turned = [jnp.transpose(jnp.concatenate(flat[k : k + group], axis=0)) for k in range(0, tiles, group)]
        values = [t[at : at + width] for t in turned for at in (0, LANES // 2)]
        values = jnp.concatenate(values, axis=1).astype(BF16)
        digits = jnp.transpose(flat[tiles])
        places = [2 * (k + g) + half for k in range(0, tiles, group) for half in (0, 1) for g in range(group)]
        high = jnp.concatenate([digits[p * span : p * span + 1] for p in places], axis=1)
        low = jnp.concatenate([digits[p * span + span // 2 : p * span + span // 2 + 1] for p in places], axis=1)
        hot = (low.astype(I32) == iota((DIGIT, low.shape[1]), 0)).astype(F32).astype(BF16)
        kept = [values * (high == float(h)).astype(F32).astype(BF16) for h in range(rows // DIGIT)]
        return dot(jnp.concatenate(kept, axis=0), hot, (1, 1))

    def store(sums, add):
        for h in range(rows // DIGIT):
            piece = sums[h * width : (h + 1) * width]
            at = slice(h * DIGIT, (h + 1) * DIGIT)
            out_ref[:, at] = out_ref[:, at] + piece if add else piece

    store(part(0), False)
    if devices > step:

        def more(i, _):
            store(part(i), True)
            return 0

        lax.fori_loop(1, devices // step, more, 0)
    moves.append(pltpu.make_async_copy(out_ref, sums_hbm, sems.at[2]))
    moves[-1].start()
    for move in moves:
        move.wait()


def body(ent_table, panels, rel_vecs, head_slots, tail_slots, negatives, requests, block_count):
    shards = lax.axis_size("entity")
    buckets = lax.axis_size("bucket")
    shard_rows, features = ent_table.shape
    cap = requests.shape[2]
    total = shards * cap
    width = features // buckets

    def swap(x, s):
        return lax.ppermute(x, "entity", [(i, i ^ s) for i in range(shards)])

    def out(shape, dtype=F32):
        return jax.ShapeDtypeStruct(shape, dtype)

    def like(x):
        return out(x.shape, x.dtype)

    vmem, hbm = pltpu.VMEM, pltpu.HBM
    asked = [swap(requests, s) for s in range(3, shards, 2)]
    other = swap(ent_table, 1)
    edges, pairs, rows, own, table, panel, rel = call(
        prepare_kernel,
        [pltpu.SMEM] + [hbm] * 7,
        [out((total, 2 * total)), out((total, 2 * total)), out((shards, FOLD, LANES))]
        + [like(x) for x in (requests, ent_table, panels, rel_vecs)],
        [
            pltpu.VMEM(head_slots.shape, I32),
            pltpu.VMEM(tail_slots.shape, I32),
            pltpu.VMEM(negatives.shape, I32),
            pltpu.SemaphoreType.DMA((7,)),
        ],
    )(
        block_count,
        *[
            pltpu.with_memory_space_constraint(x, hbm)
            for x in (head_slots, tail_slots, negatives, requests, ent_table, panels, rel_vecs)
        ]
    )

    def pick(first, ids):
        kernel = functools.partial(pick_kernel, first)
        return call(kernel, [vmem] * 3, [out((2 * cap, features), BF16)])(table, other, ids)[0]

    found = [pick(1, ids) for ids in asked]
    parts = [pick(0, own)] + [swap(x, 2 * c + 3) for c, x in enumerate(found)]
    devices = buckets * shards
    stride = devices - 5
    order = [p * stride % devices for p in range(devices)]
    turned, near_centers, near_proj = call(
        near_kernel,
        [vmem] * 3,
        [out((features, features), BF16), out((2 * cap, features), BF16), out((2 * cap, features), BF16)],
    )(panel, rel, parts[0])
    send, panel_grad, rel_grad = call(
        functools.partial(terms_kernel, buckets, negatives.shape[2], pow(stride, -1, devices)),
        [vmem] * (8 + len(parts)),
        [out((devices, cap // (2 * FOLD) + 1, FOLD, LANES), BF16), out((features, features)), out((1, features))],
    )(panel, turned, rel, edges, pairs, rows, near_centers, near_proj, *parts)
    got = lax.all_to_all(
        send, ("bucket", "entity"), split_axis=0, concat_axis=0, tiled=True, axis_index_groups=[order]
    )
    ent_grad, panel_grad, rel_grad = call(
        functools.partial(finish_kernel, width),
        [vmem] * 3,
        [out((width, shard_rows)), out((1, features, features)), out((1, features))],
        [
            pltpu.VMEM((width, shard_rows), F32),
            pltpu.SemaphoreType.DMA((3,)),
        ],
        hbm,
    )(got, panel_grad, rel_grad)
    return ent_grad.T, panel_grad, rel_grad


def solution(mesh):
    both = ("bucket", "entity")
    placed = (
        P("entity", None),
        P(both, None, None),
        P(both, None),
        P(both, None, None),
        P(both, None, None),
        P(both, None, None),
        P(both, None, None),
        P(both),
    )
    return jax.shard_map(
        body,
        mesh=mesh,
        in_specs=placed,
        out_specs=(P("entity", "bucket"), P(both, None, None), P(both, None)),
        check_vma=False,
    )
```

```python
import functools

import jax
import jax.numpy as jnp
from jax import lax
from jax.experimental import pallas as pl
from jax.experimental.pallas import tpu as pltpu
from jax.sharding import PartitionSpec as P

MARGIN = 2.0
LANES = 128
FOLD = 4
DIGIT = 256
F32 = jnp.float32
BF16 = jnp.bfloat16
I32 = jnp.int32
VMEM_BYTES = 16 * 1024 * 1024


def dot(a, b, over):
    return lax.dot_general(a, b, ((over[:1], over[1:]), ((), ())), preferred_element_type=F32)


def iota(shape, axis):
    return lax.broadcasted_iota(I32, shape, axis)


def flip(column):
    n = column.shape[0]
    return jnp.sum(jnp.where(iota((n, n), 0) == iota((n, n), 1), column, 0.0), axis=0, keepdims=True)


def call(kernel, ins, outs, scratch=(), space=pltpu.VMEM):
    return pl.pallas_call(
        kernel,
        out_shape=outs,
        in_specs=[pl.BlockSpec(memory_space=place) for place in ins],
        out_specs=[pl.BlockSpec(memory_space=space)] * len(outs),
        scratch_shapes=list(scratch),
        compiler_params=pltpu.CompilerParams(vmem_limit_bytes=VMEM_BYTES),
    )


def prepare_kernel(
    count_ref, head_hbm, tail_hbm, neg_hbm, req_hbm, table_hbm, panel_hbm, rel_hbm,
    edges_ref, pairs_ref, rows_ref, req_ref, table_ref, panel_ref, rel_ref,
    head_ref, tail_ref, neg_ref, sems,
):
    moves = [
        pltpu.make_async_copy(src, dst, sems.at[i])
        for i, (src, dst) in enumerate(
            [
                (head_hbm, head_ref),
                (tail_hbm, tail_ref),
                (neg_hbm, neg_ref),
                (req_hbm, req_ref),
                (rel_hbm, rel_ref),
                (table_hbm, table_ref),
                (panel_hbm, panel_ref),
            ]
        )
    ]
    for move in moves:
        move.start()
    for move in moves[:4]:
        move.wait()
    shards, cap = req_ref.shape[1:]
    total = shards * cap
    me = lax.axis_index("entity")
    blocks, edge = head_ref.shape[1:]
    negs = neg_ref.shape[2]
    live_blocks = count_ref[0]
    edges = jnp.zeros((2 * total, 2 * total), F32)
    pairs = jnp.zeros((total, 2 * total), F32)
    left = iota(pairs.shape, 1) < total
    edge_slot = jnp.bitwise_xor(iota((total, edge), 0), me * cap)
    neg_slot = jnp.bitwise_xor(iota((total, negs), 0), me * cap)
    for j in range(blocks):
        live = (j < live_blocks).astype(F32)
        head = (head_ref[0, j : j + 1, :] == edge_slot).astype(F32) * live
        tail = (tail_ref[0, j : j + 1, :] == edge_slot).astype(F32)
        neg = (neg_ref[0, j : j + 1, :] == neg_slot).astype(F32)
        ends = jnp.concatenate([head, tail], axis=0).astype(BF16)
        edges += dot(ends, ends, (1, 1))
        heads = jnp.sum(head, axis=1, keepdims=True)
        others = jnp.sum(neg, axis=1, keepdims=True)
        pairs += jnp.where(left, others, heads) * flip(jnp.concatenate([heads, others], axis=0))
    edges_ref[...] = jnp.where(left, edges[total:], edges[:total])
    pairs_ref[...] = pairs
    numbers = jnp.concatenate([req_ref[0, pl.ds(jnp.bitwise_xor(me, s), 1), :] for s in range(shards)], axis=0)
    lane = iota((shards, LANES), 1)
    span = LANES // (cap // FOLD)
    for i in range(FOLD):
        spread = jnp.zeros((shards, LANES), I32)
        for k in range(cap // FOLD):
            spread = jnp.where(lane // span == k, numbers[:, k * FOLD + i : k * FOLD + i + 1], spread)
        digit = jnp.where(lane % span < span // 2, spread // DIGIT, spread % DIGIT)
        rows_ref[:, i, :] = digit.astype(F32)
    for move in moves[4:]:
        move.wait()


def pick_kernel(first, near_ref, other_ref, asked_ref, out_ref):
    me = lax.axis_index("entity")
    cap = asked_ref.shape[2]
    for k, table_ref in enumerate((near_ref, other_ref)):
        asked = asked_ref[0, pl.ds(jnp.bitwise_xor(me, k), 1), :]
        hot = (asked == iota((table_ref.shape[0], cap), 0)).astype(F32).astype(BF16)
        at = (first ^ k) * cap
        out_ref[at : at + cap] = dot(hot, table_ref[...], (0, 0)).astype(BF16)


def project(rows, turned, relation):
    proj = dot(rows, turned, (1, 0)).astype(BF16)
    return (proj.astype(F32) + relation.astype(F32)).astype(BF16), proj


def near_kernel(panel_ref, rel_ref, rows_ref, turned_ref, centers_ref, proj_ref):
    turned_ref[...] = jnp.transpose(panel_ref[0])
    centers_ref[...], proj_ref[...] = project(rows_ref[...], turned_ref[...], rel_ref[...])


def terms_kernel(buckets, negs, place, *refs):
    panel_ref, turned_ref, rel_ref, edges_ref, pairs_ref, rows_ref, near_centers, near_proj = refs[:8]
    send_ref, panel_grad_ref, rel_grad_ref = refs[-3:]
    parts = refs[8:-3]
    fetched = jnp.concatenate([r[...] for r in parts], axis=0)
    far_centers, far_proj = project(fetched[near_proj.shape[0] :], turned_ref[...], rel_ref[...])
    proj = jnp.concatenate([near_proj[...], far_proj], axis=0)
    centers = jnp.concatenate([near_centers[...], far_centers], axis=0)
    proj_f = proj.astype(F32)
    center_f = centers.astype(F32)
    total, features = proj.shape
    points = jnp.concatenate([centers, proj], axis=0)
    gram = dot(points, points, (1, 1))
    norms = jnp.concatenate(
        [jnp.sum(x * x, axis=1, keepdims=True) for x in (center_f, proj_f)], axis=0
    )
    left = iota((total, 2 * total), 1) < total
    dist = (
        jnp.where(left, norms[total:], norms[:total])
        + flip(norms)
        - 2.0 * jnp.where(left, gram[total:], gram[:total])
    )
    pos = edges_ref[...] * jax.nn.sigmoid(dist - MARGIN)
    neg = -jax.nn.sigmoid(MARGIN - dist) * (1.0 / negs)
    exact = pos + pairs_ref[...] * neg
    rounded = pos + pairs_ref[...] * neg.astype(BF16).astype(F32)
    high = rounded.astype(BF16)
    low = (rounded - high.astype(F32)).astype(BF16)
    mixed = dot(jnp.concatenate([high, low], axis=0), points, (1, 0))
    from_centers = jnp.sum(jnp.where(left, 0.0, exact), axis=1, keepdims=True) * center_f
    from_others = jnp.sum(jnp.where(left, exact, 0.0), axis=1, keepdims=True) * proj_f
    grad = (2.0 * (from_centers + from_others - mixed[:total] - mixed[total:])).astype(BF16)
    grad_rows = dot(grad, panel_ref[0], (1, 0))
    panel_grad_ref[...] = dot(grad, fetched, (0, 0))
    devices, tiles, _, _ = send_ref.shape
    shards = devices // buckets
    tiles -= 1
    width = features // buckets
    me = lax.axis_index("entity")
    lane = iota((total, LANES), 1)
    rows = rows_ref[...].astype(BF16)
    for b in range(buckets):
        block, offset = divmod(b * width, LANES)
        piece = grad_rows[:, block * LANES : (block + 1) * LANES]
        near = pltpu.roll(piece, LANES - offset, 1) if offset else piece
        far = pltpu.roll(piece, (LANES + LANES // 2 - offset) % LANES, 1) if offset != LANES // 2 else piece
        far = pltpu.roll(far, total - FOLD, 0)
        piece = jnp.where(lane < LANES // 2, near, far).reshape(total // (2 * FOLD), 2 * FOLD, LANES)
        piece = piece[:, :FOLD].astype(BF16)
        for s in range(shards):
            to = lax.rem((b * shards + jnp.bitwise_xor(me, s ^ 1)) * place, devices)
            send_ref[to, :tiles] = piece[s * tiles : (s + 1) * tiles]
            send_ref[to, tiles] = rows[s]
    from_others = jnp.sum(jnp.where(left, rounded, 0.0), axis=1, keepdims=True) * proj_f
    rel_grad_ref[...] = 2.0 * jnp.sum(from_centers - from_others, axis=0, keepdims=True)


def finish_kernel(width, got_ref, panel_ref, rel_grad_ref, sums_hbm, panel_hbm, rel_hbm, out_ref, sems):
    moves = [
        pltpu.make_async_copy(panel_ref, panel_hbm.at[0], sems.at[0]),
        pltpu.make_async_copy(rel_grad_ref, rel_hbm, sems.at[1]),
    ]
    for move in moves:
        move.start()
    devices, tiles, _, _ = got_ref.shape
    tiles -= 1
    rows = out_ref.shape[1]
    step = min(devices, 32)
    span = LANES // (2 * tiles)

    def part(i):
        got = got_ref[pl.ds(i * step, step)].astype(F32)
        flat = [got[:, k].reshape(step * FOLD, LANES) for k in range(tiles + 1)]
        group = max(1, LANES // (step * FOLD))
        turned = [jnp.transpose(jnp.concatenate(flat[k : k + group], axis=0)) for k in range(0, tiles, group)]
        values = [t[at : at + width] for t in turned for at in (0, LANES // 2)]
        values = jnp.concatenate(values, axis=1).astype(BF16)
        digits = jnp.transpose(flat[tiles])
        places = [2 * (k + g) + half for k in range(0, tiles, group) for half in (0, 1) for g in range(group)]
        high = jnp.concatenate([digits[p * span : p * span + 1] for p in places], axis=1)
        low = jnp.concatenate([digits[p * span + span // 2 : p * span + span // 2 + 1] for p in places], axis=1)
        hot = (low.astype(I32) == iota((DIGIT, low.shape[1]), 0)).astype(F32).astype(BF16)
        kept = [values * (high == float(h)).astype(F32).astype(BF16) for h in range(rows // DIGIT)]
        return dot(jnp.concatenate(kept, axis=0), hot, (1, 1))

    def store(sums, add):
        for h in range(rows // DIGIT):
            piece = sums[h * width : (h + 1) * width]
            at = slice(h * DIGIT, (h + 1) * DIGIT)
            out_ref[:, at] = out_ref[:, at] + piece if add else piece

    store(part(0), False)
    if devices > step:

        def more(i, _):
            store(part(i), True)
            return 0

        lax.fori_loop(1, devices // step, more, 0)
    moves.append(pltpu.make_async_copy(out_ref, sums_hbm, sems.at[2]))
    moves[-1].start()
    for move in moves:
        move.wait()


def body(ent_table, panels, rel_vecs, head_slots, tail_slots, negatives, requests, block_count):
    shards = lax.axis_size("entity")
    buckets = lax.axis_size("bucket")
    shard_rows, features = ent_table.shape
    cap = requests.shape[2]
    total = shards * cap
    width = features // buckets

    def swap(x, s):
        return lax.ppermute(x, "entity", [(i, i ^ s) for i in range(shards)])

    def out(shape, dtype=F32):
        return jax.ShapeDtypeStruct(shape, dtype)

    def like(x):
        return out(x.shape, x.dtype)

    vmem, hbm = pltpu.VMEM, pltpu.HBM
    asked = [swap(requests, s) for s in range(3, shards, 2)]
    other = swap(ent_table, 1)
    edges, pairs, rows, own, table, panel, rel = call(
        prepare_kernel,
        [pltpu.SMEM] + [hbm] * 7,
        [out((total, 2 * total)), out((total, 2 * total)), out((shards, FOLD, LANES))]
        + [like(x) for x in (requests, ent_table, panels, rel_vecs)],
        [
            pltpu.VMEM(head_slots.shape, I32),
            pltpu.VMEM(tail_slots.shape, I32),
            pltpu.VMEM(negatives.shape, I32),
            pltpu.SemaphoreType.DMA((7,)),
        ],
    )(
        block_count,
        *[
            pltpu.with_memory_space_constraint(x, hbm)
            for x in (head_slots, tail_slots, negatives, requests, ent_table, panels, rel_vecs)
        ]
    )

    def pick(first, ids):
        kernel = functools.partial(pick_kernel, first)
        return call(kernel, [vmem] * 3, [out((2 * cap, features), BF16)])(table, other, ids)[0]

    found = [pick(1, ids) for ids in asked]
    parts = [pick(0, own)] + [swap(x, 2 * c + 3) for c, x in enumerate(found)]
    devices = buckets * shards
    stride = devices - 5
    order = [p * stride % devices ^ 1 for p in range(devices)]
    turned, near_centers, near_proj = call(
        near_kernel,
        [vmem] * 3,
        [out((features, features), BF16), out((2 * cap, features), BF16), out((2 * cap, features), BF16)],
    )(panel, rel, parts[0])
    send, panel_grad, rel_grad = call(
        functools.partial(terms_kernel, buckets, negatives.shape[2], pow(stride, -1, devices)),
        [vmem] * (8 + len(parts)),
        [out((devices, cap // (2 * FOLD) + 1, FOLD, LANES), BF16), out((features, features)), out((1, features))],
    )(panel, turned, rel, edges, pairs, rows, near_centers, near_proj, *parts)
    got = lax.all_to_all(
        send, ("bucket", "entity"), split_axis=0, concat_axis=0, tiled=True, axis_index_groups=[order]
    )
    ent_grad, panel_grad, rel_grad = call(
        functools.partial(finish_kernel, width),
        [vmem] * 3,
        [out((width, shard_rows)), out((1, features, features)), out((1, features))],
        [
            pltpu.VMEM((width, shard_rows), F32),
            pltpu.SemaphoreType.DMA((3,)),
        ],
        hbm,
    )(got, panel_grad, rel_grad)
    return ent_grad.T, panel_grad, rel_grad


def solution(mesh):
    both = ("bucket", "entity")
    placed = (
        P("entity", None),
        P(both, None, None),
        P(both, None),
        P(both, None, None),
        P(both, None, None),
        P(both, None, None),
        P(both, None, None),
        P(both),
    )
    return jax.shard_map(
        body,
        mesh=mesh,
        in_specs=placed,
        out_specs=(P("entity", "bucket"), P(both, None, None), P(both, None)),
        check_vma=False,
    )
```

```python
import functools

import jax
import jax.numpy as jnp
from jax import lax
from jax.experimental import pallas as pl
from jax.experimental.pallas import tpu as pltpu
from jax.sharding import PartitionSpec as P

MARGIN = 2.0
LANES = 128
FOLD = 4
COPIES = 2
DIGIT = 256
F32 = jnp.float32
BF16 = jnp.bfloat16
I32 = jnp.int32
VMEM_BYTES = 16 * 1024 * 1024


def dot(a, b, over):
    return lax.dot_general(a, b, ((over[:1], over[1:]), ((), ())), preferred_element_type=F32)


def iota(shape, axis):
    return lax.broadcasted_iota(I32, shape, axis)


def flip(column):
    n = column.shape[0]
    return jnp.sum(jnp.where(iota((n, n), 0) == iota((n, n), 1), column, 0.0), axis=0, keepdims=True)


def call(kernel, ins, outs, scratch=(), space=pltpu.VMEM):
    return pl.pallas_call(
        kernel,
        out_shape=outs,
        in_specs=[pl.BlockSpec(memory_space=place) for place in ins],
        out_specs=[pl.BlockSpec(memory_space=space)] * len(outs),
        scratch_shapes=list(scratch),
        compiler_params=pltpu.CompilerParams(vmem_limit_bytes=VMEM_BYTES),
    )


def prepare_kernel(
    count_ref, head_hbm, tail_hbm, neg_hbm, req_hbm, table_hbm, panel_hbm, rel_hbm,
    edges_ref, pairs_ref, rows_ref, req_ref, table_ref, panel_ref, rel_ref,
    head_ref, tail_ref, neg_ref, sems,
):
    moves = [
        pltpu.make_async_copy(src, dst, sems.at[i])
        for i, (src, dst) in enumerate(
            [
                (head_hbm, head_ref),
                (tail_hbm, tail_ref),
                (neg_hbm, neg_ref),
                (req_hbm, req_ref),
                (rel_hbm, rel_ref),
                (table_hbm, table_ref),
                (panel_hbm, panel_ref),
            ]
        )
    ]
    for move in moves:
        move.start()
    for move in moves[:4]:
        move.wait()
    shards, cap = req_ref.shape[1:]
    total = shards * cap
    me = lax.axis_index("entity")
    blocks, edge = head_ref.shape[1:]
    negs = neg_ref.shape[2]
    live_blocks = count_ref[0]
    edges = jnp.zeros((2 * total, 2 * total), F32)
    pairs = jnp.zeros((total, 2 * total), F32)
    left = iota(pairs.shape, 1) < total
    edge_slot = jnp.bitwise_xor(iota((total, edge), 0), me * cap)
    neg_slot = jnp.bitwise_xor(iota((total, negs), 0), me * cap)
    for j in range(blocks):
        live = (j < live_blocks).astype(F32)
        head = (head_ref[0, j : j + 1, :] == edge_slot).astype(F32) * live
        tail = (tail_ref[0, j : j + 1, :] == edge_slot).astype(F32)
        neg = (neg_ref[0, j : j + 1, :] == neg_slot).astype(F32)
        ends = jnp.concatenate([head, tail], axis=0).astype(BF16)
        edges += dot(ends, ends, (1, 1))
        heads = jnp.sum(head, axis=1, keepdims=True)
        others = jnp.sum(neg, axis=1, keepdims=True)
        pairs += jnp.where(left, others, heads) * flip(jnp.concatenate([heads, others], axis=0))
    edges_ref[...] = jnp.where(left, edges[total:], edges[:total])
    pairs_ref[...] = pairs
    numbers = jnp.concatenate([req_ref[0, pl.ds(jnp.bitwise_xor(me, s), 1), :] for s in range(shards)], axis=0)
    lane = iota((shards, LANES), 1)
    span = LANES // (cap // FOLD)
    for i in range(FOLD):
        spread = jnp.zeros((shards, LANES), I32)
        for k in range(cap // FOLD):
            spread = jnp.where(lane // span == k, numbers[:, k * FOLD + i : k * FOLD + i + 1], spread)
        digit = jnp.where(lane % span < span // 2, spread // DIGIT, spread % DIGIT)
        rows_ref[:, i, :] = digit.astype(F32)
    for move in moves[4:]:
        move.wait()


def pick_kernel(first, near_ref, other_ref, asked_ref, out_ref):
    me = lax.axis_index("entity")
    cap = asked_ref.shape[2]
    for k, table_ref in enumerate((near_ref, other_ref)):
        asked = asked_ref[0, pl.ds(jnp.bitwise_xor(me, k), 1), :]
        hot = (asked == iota((table_ref.shape[0], cap), 0)).astype(F32).astype(BF16)
        at = (first ^ k) * cap
        out_ref[at : at + cap] = dot(hot, table_ref[...], (0, 0)).astype(BF16)


def project(rows, turned, relation):
    proj = dot(rows, turned, (1, 0)).astype(BF16)
    return (proj.astype(F32) + relation.astype(F32)).astype(BF16), proj


def near_kernel(panel_ref, rel_ref, rows_ref, turned_ref, centers_ref, proj_ref):
    turned_ref[...] = jnp.transpose(panel_ref[0])
    centers_ref[...], proj_ref[...] = project(rows_ref[...], turned_ref[...], rel_ref[...])


def terms_kernel(buckets, negs, place, *refs):
    panel_ref, turned_ref, rel_ref, edges_ref, pairs_ref, rows_ref, near_centers, near_proj = refs[:8]
    send_ref, panel_grad_ref, rel_grad_ref = refs[-3:]
    parts = refs[8:-3]
    fetched = jnp.concatenate([r[...] for r in parts], axis=0)
    far_centers, far_proj = project(fetched[near_proj.shape[0] :], turned_ref[...], rel_ref[...])
    proj = jnp.concatenate([near_proj[...], far_proj], axis=0)
    centers = jnp.concatenate([near_centers[...], far_centers], axis=0)
    proj_f = proj.astype(F32)
    center_f = centers.astype(F32)
    total, features = proj.shape
    points = jnp.concatenate([centers, proj], axis=0)
    gram = dot(points, points, (1, 1))
    norms = jnp.concatenate(
        [jnp.sum(x * x, axis=1, keepdims=True) for x in (center_f, proj_f)], axis=0
    )
    left = iota((total, 2 * total), 1) < total
    dist = (
        jnp.where(left, norms[total:], norms[:total])
        + flip(norms)
        - 2.0 * jnp.where(left, gram[total:], gram[:total])
    )
    pos = edges_ref[...] * jax.nn.sigmoid(dist - MARGIN)
    neg = -jax.nn.sigmoid(MARGIN - dist) * (1.0 / negs)
    exact = pos + pairs_ref[...] * neg
    rounded = pos + pairs_ref[...] * neg.astype(BF16).astype(F32)
    high = rounded.astype(BF16)
    low = (rounded - high.astype(F32)).astype(BF16)
    mixed = dot(jnp.concatenate([high, low], axis=0), points, (1, 0))
    from_centers = jnp.sum(jnp.where(left, 0.0, exact), axis=1, keepdims=True) * center_f
    from_others = jnp.sum(jnp.where(left, exact, 0.0), axis=1, keepdims=True) * proj_f
    grad = (2.0 * (from_centers + from_others - mixed[:total] - mixed[total:])).astype(BF16)
    grad_rows = dot(grad, panel_ref[0], (1, 0))
    panel_grad_ref[...] = dot(grad, fetched, (0, 0))
    devices, tiles, _, _ = send_ref.shape
    shards = devices // buckets
    tiles -= 1
    width = features // buckets
    me = lax.axis_index("entity")
    lane = iota((total, LANES), 1)
    rows = rows_ref[...].astype(BF16)
    for b in range(buckets):
        block, offset = divmod(b * width, LANES)
        piece = grad_rows[:, block * LANES : (block + 1) * LANES]
        near = pltpu.roll(piece, LANES - offset, 1) if offset else piece
        far = pltpu.roll(piece, (LANES + LANES // 2 - offset) % LANES, 1) if offset != LANES // 2 else piece
        far = pltpu.roll(far, total - FOLD, 0)
        piece = jnp.where(lane < LANES // 2, near, far).reshape(total // (2 * FOLD), 2 * FOLD, LANES)
        piece = piece[:, :FOLD].astype(BF16)
        for s in range(shards):
            to = lax.rem((b * shards + jnp.bitwise_xor(me, s ^ 1)) * place, devices)
            send_ref[to, :tiles] = piece[s * tiles : (s + 1) * tiles]
            send_ref[to, tiles] = rows[s]
    from_others = jnp.sum(jnp.where(left, rounded, 0.0), axis=1, keepdims=True) * proj_f
    rel_grad_ref[...] = 2.0 * jnp.sum(from_centers - from_others, axis=0, keepdims=True)


def finish_kernel(width, got_ref, panel_ref, rel_grad_ref, sums_hbm, panel_hbm, rel_hbm, out_ref, sems):
    def copies(source, target, first):
        step = source.shape[0] // COPIES
        at = [pl.ds(i * step, step) for i in range(COPIES)]
        return [pltpu.make_async_copy(source.at[a], target.at[a], sems.at[first + i]) for i, a in enumerate(at)]

    moves = copies(panel_ref, panel_hbm.at[0], 1) + [pltpu.make_async_copy(rel_grad_ref, rel_hbm, sems.at[0])]
    for move in moves:
        move.start()
    devices, tiles, _, _ = got_ref.shape
    tiles -= 1
    rows = out_ref.shape[1]
    step = min(devices, 32)
    span = LANES // (2 * tiles)

    def part(i):
        got = got_ref[pl.ds(i * step, step)].astype(F32)
        flat = [got[:, k].reshape(step * FOLD, LANES) for k in range(tiles + 1)]
        group = max(1, LANES // (step * FOLD))
        turned = [jnp.transpose(jnp.concatenate(flat[k : k + group], axis=0)) for k in range(0, tiles, group)]
        values = [t[at : at + width] for t in turned for at in (0, LANES // 2)]
        values = jnp.concatenate(values, axis=1).astype(BF16)
        digits = jnp.transpose(flat[tiles])
        places = [2 * (k + g) + half for k in range(0, tiles, group) for half in (0, 1) for g in range(group)]
        high = jnp.concatenate([digits[p * span : p * span + 1] for p in places], axis=1)
        low = jnp.concatenate([digits[p * span + span // 2 : p * span + span // 2 + 1] for p in places], axis=1)
        hot = (low.astype(I32) == iota((DIGIT, low.shape[1]), 0)).astype(F32).astype(BF16)
        kept = [values * (high == float(h)).astype(F32).astype(BF16) for h in range(rows // DIGIT)]
        return dot(jnp.concatenate(kept, axis=0), hot, (1, 1))

    def store(sums, add):
        for h in range(rows // DIGIT):
            piece = sums[h * width : (h + 1) * width]
            at = slice(h * DIGIT, (h + 1) * DIGIT)
            out_ref[:, at] = out_ref[:, at] + piece if add else piece

    store(part(0), False)
    if devices > step:

        def more(i, _):
            store(part(i), True)
            return 0

        lax.fori_loop(1, devices // step, more, 0)
    last = copies(out_ref, sums_hbm, 1 + COPIES)
    for move in last:
        move.start()
    moves += last
    for move in moves:
        move.wait()


def body(ent_table, panels, rel_vecs, head_slots, tail_slots, negatives, requests, block_count):
    shards = lax.axis_size("entity")
    buckets = lax.axis_size("bucket")
    shard_rows, features = ent_table.shape
    cap = requests.shape[2]
    total = shards * cap
    width = features // buckets

    def swap(x, s):
        return lax.ppermute(x, "entity", [(i, i ^ s) for i in range(shards)])

    def out(shape, dtype=F32):
        return jax.ShapeDtypeStruct(shape, dtype)

    def like(x):
        return out(x.shape, x.dtype)

    vmem, hbm = pltpu.VMEM, pltpu.HBM
    asked = [swap(requests, s) for s in range(3, shards, 2)]
    other = swap(ent_table, 1)
    edges, pairs, rows, own, table, panel, rel = call(
        prepare_kernel,
        [pltpu.SMEM] + [hbm] * 7,
        [out((total, 2 * total)), out((total, 2 * total)), out((shards, FOLD, LANES))]
        + [like(x) for x in (requests, ent_table, panels, rel_vecs)],
        [
            pltpu.VMEM(head_slots.shape, I32),
            pltpu.VMEM(tail_slots.shape, I32),
            pltpu.VMEM(negatives.shape, I32),
            pltpu.SemaphoreType.DMA((7,)),
        ],
    )(
        block_count,
        *[
            pltpu.with_memory_space_constraint(x, hbm)
            for x in (head_slots, tail_slots, negatives, requests, ent_table, panels, rel_vecs)
        ]
    )

    def pick(first, ids):
        kernel = functools.partial(pick_kernel, first)
        return call(kernel, [vmem] * 3, [out((2 * cap, features), BF16)])(table, other, ids)[0]

    found = [pick(1, ids) for ids in asked]
    parts = [pick(0, own)] + [swap(x, 2 * c + 3) for c, x in enumerate(found)]
    devices = buckets * shards
    stride = devices - 5
    order = [p * stride % devices ^ 1 for p in range(devices)]
    turned, near_centers, near_proj = call(
        near_kernel,
        [vmem] * 3,
        [out((features, features), BF16), out((2 * cap, features), BF16), out((2 * cap, features), BF16)],
    )(panel, rel, parts[0])
    send, panel_grad, rel_grad = call(
        functools.partial(terms_kernel, buckets, negatives.shape[2], pow(stride, -1, devices)),
        [vmem] * (8 + len(parts)),
        [out((devices, cap // (2 * FOLD) + 1, FOLD, LANES), BF16), out((features, features)), out((1, features))],
    )(panel, turned, rel, edges, pairs, rows, near_centers, near_proj, *parts)
    got = lax.all_to_all(
        send, ("bucket", "entity"), split_axis=0, concat_axis=0, tiled=True, axis_index_groups=[order]
    )
    ent_grad, panel_grad, rel_grad = call(
        functools.partial(finish_kernel, width),
        [vmem] * 3,
        [out((width, shard_rows)), out((1, features, features)), out((1, features))],
        [
            pltpu.VMEM((width, shard_rows), F32),
            pltpu.SemaphoreType.DMA((1 + 2 * COPIES,)),
        ],
        hbm,
    )(got, panel_grad, rel_grad)
    return ent_grad.T, panel_grad, rel_grad


def solution(mesh):
    both = ("bucket", "entity")
    placed = (
        P("entity", None),
        P(both, None, None),
        P(both, None),
        P(both, None, None),
        P(both, None, None),
        P(both, None, None),
        P(both, None, None),
        P(both),
    )
    return jax.shard_map(
        body,
        mesh=mesh,
        in_specs=placed,
        out_specs=(P("entity", "bucket"), P(both, None, None), P(both, None)),
        check_vma=False,
    )
```

```python
import functools

import jax
import jax.numpy as jnp
from jax import lax
from jax.experimental import pallas as pl
from jax.experimental.pallas import tpu as pltpu
from jax.sharding import PartitionSpec as P

MARGIN = 2.0
LANES = 128
FOLD = 2
DIGIT = 256
F32 = jnp.float32
BF16 = jnp.bfloat16
I32 = jnp.int32
VMEM_BYTES = 16 * 1024 * 1024


def dot(a, b, over):
    return lax.dot_general(a, b, ((over[:1], over[1:]), ((), ())), preferred_element_type=F32)


def iota(shape, axis):
    return lax.broadcasted_iota(I32, shape, axis)


def flip(column):
    n = column.shape[0]
    return jnp.sum(jnp.where(iota((n, n), 0) == iota((n, n), 1), column, 0.0), axis=0, keepdims=True)


def call(kernel, ins, outs, scratch=(), space=pltpu.VMEM):
    return pl.pallas_call(
        kernel,
        out_shape=outs,
        in_specs=[pl.BlockSpec(memory_space=place) for place in ins],
        out_specs=[pl.BlockSpec(memory_space=space)] * len(outs),
        scratch_shapes=list(scratch),
        compiler_params=pltpu.CompilerParams(vmem_limit_bytes=VMEM_BYTES),
    )


def prepare_kernel(
    count_ref, head_hbm, tail_hbm, neg_hbm, req_hbm, table_hbm, panel_hbm, rel_hbm,
    edges_ref, pairs_ref, rows_ref, req_ref, table_ref, panel_ref, rel_ref,
    head_ref, tail_ref, neg_ref, sems,
):
    moves = [
        pltpu.make_async_copy(src, dst, sems.at[i])
        for i, (src, dst) in enumerate(
            [
                (head_hbm, head_ref),
                (tail_hbm, tail_ref),
                (neg_hbm, neg_ref),
                (req_hbm, req_ref),
                (rel_hbm, rel_ref),
                (table_hbm, table_ref),
                (panel_hbm, panel_ref),
            ]
        )
    ]
    for move in moves:
        move.start()
    for move in moves[:4]:
        move.wait()
    shards, cap = req_ref.shape[1:]
    total = shards * cap
    me = lax.axis_index("entity")
    blocks, edge = head_ref.shape[1:]
    negs = neg_ref.shape[2]
    live_blocks = count_ref[0]
    edges = jnp.zeros((2 * total, 2 * total), F32)
    pairs = jnp.zeros((total, 2 * total), F32)
    left = iota(pairs.shape, 1) < total
    edge_slot = jnp.bitwise_xor(iota((total, edge), 0), me * cap)
    neg_slot = jnp.bitwise_xor(iota((total, negs), 0), me * cap)
    for j in range(blocks):
        live = (j < live_blocks).astype(F32)
        head = (head_ref[0, j : j + 1, :] == edge_slot).astype(F32) * live
        tail = (tail_ref[0, j : j + 1, :] == edge_slot).astype(F32)
        neg = (neg_ref[0, j : j + 1, :] == neg_slot).astype(F32)
        ends = jnp.concatenate([head, tail], axis=0).astype(BF16)
        edges += dot(ends, ends, (1, 1))
        heads = jnp.sum(head, axis=1, keepdims=True)
        others = jnp.sum(neg, axis=1, keepdims=True)
        pairs += jnp.where(left, others, heads) * flip(jnp.concatenate([heads, others], axis=0))
    edges_ref[...] = jnp.where(left, edges[total:], edges[:total])
    pairs_ref[...] = pairs
    numbers = jnp.concatenate([req_ref[0, pl.ds(jnp.bitwise_xor(me, s), 1), :] for s in range(shards)], axis=0)
    lane = iota((shards, LANES), 1)
    span = LANES // (cap // FOLD)
    for i in range(FOLD):
        spread = jnp.zeros((shards, LANES), I32)
        for k in range(cap // FOLD):
            spread = jnp.where(lane // span == k, numbers[:, k * FOLD + i : k * FOLD + i + 1], spread)
        digit = jnp.where(lane % span < span // 2, spread // DIGIT, spread % DIGIT)
        rows_ref[:, i, :] = digit.astype(F32)
    for move in moves[4:]:
        move.wait()


def pick_kernel(first, near_ref, other_ref, asked_ref, out_ref):
    me = lax.axis_index("entity")
    cap = asked_ref.shape[2]
    for k, table_ref in enumerate((near_ref, other_ref)):
        asked = asked_ref[0, pl.ds(jnp.bitwise_xor(me, k), 1), :]
        hot = (asked == iota((table_ref.shape[0], cap), 0)).astype(F32).astype(BF16)
        at = (first ^ k) * cap
        out_ref[at : at + cap] = dot(hot, table_ref[...], (0, 0)).astype(BF16)


def project(rows, turned, relation):
    proj = dot(rows, turned, (1, 0)).astype(BF16)
    return (proj.astype(F32) + relation.astype(F32)).astype(BF16), proj


def near_kernel(panel_ref, rel_ref, rows_ref, turned_ref, centers_ref, proj_ref):
    turned_ref[...] = jnp.transpose(panel_ref[0])
    centers_ref[...], proj_ref[...] = project(rows_ref[...], turned_ref[...], rel_ref[...])


def terms_kernel(buckets, negs, place, *refs):
    panel_ref, turned_ref, rel_ref, edges_ref, pairs_ref, rows_ref, near_centers, near_proj = refs[:8]
    send_ref, panel_grad_ref, rel_grad_ref = refs[-3:]
    parts = refs[8:-3]
    fetched = jnp.concatenate([r[...] for r in parts], axis=0)
    far_centers, far_proj = project(fetched[near_proj.shape[0] :], turned_ref[...], rel_ref[...])
    proj = jnp.concatenate([near_proj[...], far_proj], axis=0)
    centers = jnp.concatenate([near_centers[...], far_centers], axis=0)
    proj_f = proj.astype(F32)
    center_f = centers.astype(F32)
    total, features = proj.shape
    points = jnp.concatenate([centers, proj], axis=0)
    gram = dot(points, points, (1, 1))
    norms = jnp.concatenate(
        [jnp.sum(x * x, axis=1, keepdims=True) for x in (center_f, proj_f)], axis=0
    )
    left = iota((total, 2 * total), 1) < total
    dist = (
        jnp.where(left, norms[total:], norms[:total])
        + flip(norms)
        - 2.0 * jnp.where(left, gram[total:], gram[:total])
    )
    pos = edges_ref[...] * jax.nn.sigmoid(dist - MARGIN)
    neg = -jax.nn.sigmoid(MARGIN - dist) * (1.0 / negs)
    exact = pos + pairs_ref[...] * neg
    rounded = pos + pairs_ref[...] * neg.astype(BF16).astype(F32)
    high = rounded.astype(BF16)
    low = (rounded - high.astype(F32)).astype(BF16)
    mixed = dot(jnp.concatenate([high, low], axis=0), points, (1, 0))
    from_centers = jnp.sum(jnp.where(left, 0.0, exact), axis=1, keepdims=True) * center_f
    from_others = jnp.sum(jnp.where(left, exact, 0.0), axis=1, keepdims=True) * proj_f
    grad = (2.0 * (from_centers + from_others - mixed[:total] - mixed[total:])).astype(BF16)
    grad_rows = dot(grad, panel_ref[0], (1, 0))
    panel_grad_ref[...] = dot(grad, fetched, (0, 0))
    devices, tiles, _, _ = send_ref.shape
    shards = devices // buckets
    tiles -= 1
    width = features // buckets
    me = lax.axis_index("entity")
    lane = iota((total, LANES), 1)
    rows = rows_ref[...].astype(BF16)
    for b in range(buckets):
        block, offset = divmod(b * width, LANES)
        piece = grad_rows[:, block * LANES : (block + 1) * LANES]
        near = pltpu.roll(piece, LANES - offset, 1) if offset else piece
        far = pltpu.roll(piece, (LANES + LANES // 2 - offset) % LANES, 1) if offset != LANES // 2 else piece
        far = pltpu.roll(far, total - FOLD, 0)
        piece = jnp.where(lane < LANES // 2, near, far).reshape(total // (2 * FOLD), 2 * FOLD, LANES)
        piece = piece[:, :FOLD].astype(BF16)
        for s in range(shards):
            to = lax.rem((b * shards + jnp.bitwise_xor(me, s ^ 1)) * place, devices)
            send_ref[to, :tiles] = piece[s * tiles : (s + 1) * tiles]
            send_ref[to, tiles] = rows[s]
    from_others = jnp.sum(jnp.where(left, rounded, 0.0), axis=1, keepdims=True) * proj_f
    rel_grad_ref[...] = 2.0 * jnp.sum(from_centers - from_others, axis=0, keepdims=True)


def finish_kernel(width, got_ref, panel_ref, rel_grad_ref, sums_hbm, panel_hbm, rel_hbm, out_ref, sems):
    moves = [
        pltpu.make_async_copy(panel_ref, panel_hbm.at[0], sems.at[0]),
        pltpu.make_async_copy(rel_grad_ref, rel_hbm, sems.at[1]),
    ]
    for move in moves:
        move.start()
    devices, tiles, _, _ = got_ref.shape
    tiles -= 1
    rows = out_ref.shape[1]
    step = min(devices, 32)
    span = LANES // (2 * tiles)

    def part(i):
        got = got_ref[pl.ds(i * step, step)].astype(F32)
        flat = [got[:, k].reshape(step * FOLD, LANES) for k in range(tiles + 1)]
        group = max(1, LANES // (step * FOLD))
        turned = [jnp.transpose(jnp.concatenate(flat[k : k + group], axis=0)) for k in range(0, tiles, group)]
        values = [t[at : at + width] for t in turned for at in (0, LANES // 2)]
        values = jnp.concatenate(values, axis=1).astype(BF16)
        digits = jnp.transpose(flat[tiles])
        places = [2 * (k + g) + half for k in range(0, tiles, group) for half in (0, 1) for g in range(group)]
        high = jnp.concatenate([digits[p * span : p * span + 1] for p in places], axis=1)
        low = jnp.concatenate([digits[p * span + span // 2 : p * span + span // 2 + 1] for p in places], axis=1)
        hot = (low.astype(I32) == iota((DIGIT, low.shape[1]), 0)).astype(F32).astype(BF16)
        kept = [values * (high == float(h)).astype(F32).astype(BF16) for h in range(rows // DIGIT)]
        return dot(jnp.concatenate(kept, axis=0), hot, (1, 1))

    def store(sums, add):
        for h in range(rows // DIGIT):
            piece = sums[h * width : (h + 1) * width]
            at = slice(h * DIGIT, (h + 1) * DIGIT)
            out_ref[:, at] = out_ref[:, at] + piece if add else piece

    store(part(0), False)
    if devices > step:

        def more(i, _):
            store(part(i), True)
            return 0

        lax.fori_loop(1, devices // step, more, 0)
    moves.append(pltpu.make_async_copy(out_ref, sums_hbm, sems.at[2]))
    moves[-1].start()
    for move in moves:
        move.wait()


def body(ent_table, panels, rel_vecs, head_slots, tail_slots, negatives, requests, block_count):
    shards = lax.axis_size("entity")
    buckets = lax.axis_size("bucket")
    shard_rows, features = ent_table.shape
    cap = requests.shape[2]
    total = shards * cap
    width = features // buckets

    def swap(x, s):
        return lax.ppermute(x, "entity", [(i, i ^ s) for i in range(shards)])

    def out(shape, dtype=F32):
        return jax.ShapeDtypeStruct(shape, dtype)

    def like(x):
        return out(x.shape, x.dtype)

    vmem, hbm = pltpu.VMEM, pltpu.HBM
    asked = [swap(requests, s) for s in range(3, shards, 2)]
    other = swap(ent_table, 1)
    edges, pairs, rows, own, table, panel, rel = call(
        prepare_kernel,
        [pltpu.SMEM] + [hbm] * 7,
        [out((total, 2 * total)), out((total, 2 * total)), out((shards, FOLD, LANES))]
        + [like(x) for x in (requests, ent_table, panels, rel_vecs)],
        [
            pltpu.VMEM(head_slots.shape, I32),
            pltpu.VMEM(tail_slots.shape, I32),
            pltpu.VMEM(negatives.shape, I32),
            pltpu.SemaphoreType.DMA((7,)),
        ],
    )(
        block_count,
        *[
            pltpu.with_memory_space_constraint(x, hbm)
            for x in (head_slots, tail_slots, negatives, requests, ent_table, panels, rel_vecs)
        ]
    )

    def pick(first, ids):
        kernel = functools.partial(pick_kernel, first)
        return call(kernel, [vmem] * 3, [out((2 * cap, features), BF16)])(table, other, ids)[0]

    found = [pick(1, ids) for ids in asked]
    parts = [pick(0, own)] + [swap(x, 2 * c + 3) for c, x in enumerate(found)]
    devices = buckets * shards
    stride = devices - 5
    order = [p * stride % devices ^ 1 for p in range(devices)]
    turned, near_centers, near_proj = call(
        near_kernel,
        [vmem] * 3,
        [out((features, features), BF16), out((2 * cap, features), BF16), out((2 * cap, features), BF16)],
    )(panel, rel, parts[0])
    send, panel_grad, rel_grad = call(
        functools.partial(terms_kernel, buckets, negatives.shape[2], pow(stride, -1, devices)),
        [vmem] * (8 + len(parts)),
        [out((devices, cap // (2 * FOLD) + 1, FOLD, LANES), BF16), out((features, features)), out((1, features))],
    )(panel, turned, rel, edges, pairs, rows, near_centers, near_proj, *parts)
    got = lax.all_to_all(
        send, ("bucket", "entity"), split_axis=0, concat_axis=0, tiled=True, axis_index_groups=[order]
    )
    ent_grad, panel_grad, rel_grad = call(
        functools.partial(finish_kernel, width),
        [vmem] * 3,
        [out((width, shard_rows)), out((1, features, features)), out((1, features))],
        [
            pltpu.VMEM((width, shard_rows), F32),
            pltpu.SemaphoreType.DMA((3,)),
        ],
        hbm,
    )(got, panel_grad, rel_grad)
    return ent_grad.T, panel_grad, rel_grad


def solution(mesh):
    both = ("bucket", "entity")
    placed = (
        P("entity", None),
        P(both, None, None),
        P(both, None),
        P(both, None, None),
        P(both, None, None),
        P(both, None, None),
        P(both, None, None),
        P(both),
    )
    return jax.shard_map(
        body,
        mesh=mesh,
        in_specs=placed,
        out_specs=(P("entity", "bucket"), P(both, None, None), P(both, None)),
        check_vma=False,
    )
```
